128 devices in a mesh: ia: 4 (over z), ja: 8 (over y_lo, x), ka: 4 (over y_hi, core).
Axes of the slice: x: 4, y: 4 (y_hi: 2, y_lo: 2; y = y_hi * 2 + y_lo), z: 4, core: 2. Of those that a mesh axis runs over, the one named last changes fastest.
Arguments:
- inputs: bfloat16 [2048, 6144], P(('ia', 'ka'), 'ja'), may hold values from -6 to 6
- up_weight: bfloat16 [6144, 24576], P('ja', ('ka', 'ia')), may hold values from -0.078125 to 0.078125
- down_weight: bfloat16 [24576, 6144], P(('ka', 'ia'), 'ja'), may hold values from -0.0390625 to 0.0390625
- out_grad: bfloat16 [2048, 6144], P(('ia', 'ka'), 'ja'), may hold values from -1.1953125 to 1.1953125
Outputs:
- output: bfloat16 [2048, 6144], P(('ia', 'ka'), 'ja')
- input_grad: bfloat16 [2048, 6144], P(('ia', 'ka'), 'ja')
- up_grad: bfloat16 [6144, 24576], P('ja', ('ka', 'ia'))
- down_grad: bfloat16 [24576, 6144], P(('ka', 'ia'), 'ja')
The draws below stay inside these ranges and needn't reach their ends.
All inputs are finite; a program needn't handle non-finite values.
Results may differ from the reference program's by a relative error of at most 0.025.
Values may be sent and summed in bfloat16 or wider, within the bound.
A program may use at most 128 MiB of HBM per device.

```python
import jax
import jax.numpy as jnp
from jax import lax

D = 6144
FF = 24576
TOK = 2048
N_IA = 4
N_JA = 8


def steps_of(own_key, dims, split, least, high):
    def one(axis_at, parts):
        heights = jax.random.uniform(jax.random.fold_in(jax.random.fold_in(own_key, 6), axis_at), (parts,), jnp.float32, least / len(split), high / len(split))
        return jnp.repeat(jnp.exp(heights), dims[axis_at] // parts).reshape((-1,) + (1,) * (len(dims) - axis_at - 1))

    gain = one(*split[0])
    for cut in split[1:]:
        gain = gain * one(*cut)
    return gain


def noise(stream_key, extent, deviation, limit, shards=(), dtype=jnp.bfloat16):
    gain = steps_of(stream_key, extent, shards, -0.22, 0.18) if shards else 1.0
    entries = jax.random.normal(stream_key, extent, jnp.float32) * deviation * gain
    return jnp.minimum(jnp.maximum(entries, -limit), limit).astype(dtype)


def setup_inputs(seed: int = 0) -> dict:
    arg_keys = jax.random.split(jax.random.key(seed), 5)
    inputs = noise(arg_keys[0], (TOK, D), 1.0, 6.0, ((0, 16), (1, 8)))
    up_weight = noise(arg_keys[1], (D, FF), D ** -0.5, 0.078125, ((0, 8), (1, 16)))
    down_weight = noise(arg_keys[2], (FF, D), FF ** -0.5, 0.0390625, ((0, 16), (1, 8)))
    out_grad = noise(arg_keys[3], (TOK, D), 0.2, 1.1953125, ((0, 16), (1, 8)))
    return dict(inputs=inputs, up_weight=up_weight, down_weight=down_weight, out_grad=out_grad)


sqrt_two_over_pi = 0.7978845608028654
cubic_coeff = 0.044715

def gelu_value(preact):
    tanh_inner = jnp.tanh(sqrt_two_over_pi * (preact + cubic_coeff * preact * preact * preact))
    return 0.5 * preact * (1.0 + tanh_inner)

def gelu_slope(preact):
    tanh_inner = jnp.tanh(sqrt_two_over_pi * (preact + cubic_coeff * preact * preact * preact))
    inner_slope = sqrt_two_over_pi * (1.0 + 3.0 * cubic_coeff * preact * preact)
    return 0.5 * (1.0 + tanh_inner) + 0.5 * preact * (1.0 - tanh_inner * tanh_inner) * inner_slope

def rounded(values):
    return lax.optimization_barrier(values.astype(jnp.bfloat16)).astype(jnp.float32)

def reference(inputs, up_weight, down_weight, out_grad):
    block_width = D // N_JA
    block_rows = TOK // N_IA
    preact = jnp.zeros((TOK, FF), jnp.float32)
    hidden_grad = jnp.zeros((TOK, FF), jnp.float32)
    for number in range(N_JA):
        lower = number * block_width
        upper = lower + block_width
        preact = preact + rounded(jnp.dot(inputs[:, lower:upper], up_weight[lower:upper, :], preferred_element_type=jnp.float32))
        hidden_grad = hidden_grad + rounded(jnp.dot(out_grad[:, lower:upper], down_weight[:, lower:upper].T, preferred_element_type=jnp.float32))
    hidden = gelu_value(preact).astype(jnp.bfloat16)
    output = jnp.dot(hidden, down_weight, preferred_element_type=jnp.float32).astype(jnp.bfloat16)
    preact_grad = (hidden_grad * gelu_slope(preact)).astype(jnp.bfloat16)
    input_grad = jnp.dot(preact_grad, up_weight.T, preferred_element_type=jnp.float32).astype(jnp.bfloat16)
    up_total = jnp.zeros((D, FF), jnp.float32)
    down_total = jnp.zeros((FF, D), jnp.float32)
    for number in range(N_IA):
        lower = number * block_rows
        upper = lower + block_rows
        up_total = up_total + rounded(jnp.dot(inputs[lower:upper].T, preact_grad[lower:upper], preferred_element_type=jnp.float32))
        down_total = down_total + rounded(jnp.dot(hidden[lower:upper].T, out_grad[lower:upper], preferred_element_type=jnp.float32))
    return (output, input_grad, up_total.astype(jnp.bfloat16), down_total.astype(jnp.bfloat16))
```

```python
import jax
import jax.numpy as jnp
from jax import lax
from jax.sharding import PartitionSpec as P

sqrt_two_over_pi = 0.7978845608028654
cubic_coeff = 0.044715
CHUNKS = 4


def gelu_value(preact):
    tanh_inner = jnp.tanh(sqrt_two_over_pi * (preact + cubic_coeff * preact * preact * preact))
    return 0.5 * preact * (1.0 + tanh_inner)


def gelu_slope(preact):
    tanh_inner = jnp.tanh(sqrt_two_over_pi * (preact + cubic_coeff * preact * preact * preact))
    inner_slope = sqrt_two_over_pi * (1.0 + 3.0 * cubic_coeff * preact * preact)
    return 0.5 * (1.0 + tanh_inner) + 0.5 * preact * (1.0 - tanh_inner * tanh_inner) * inner_slope


def contract_rows(left, right):
    return lax.dot_general(
        left, right, (((0,), (0,)), ((), ())), preferred_element_type=jnp.float32
    )


def contract_cols(left, right):
    return lax.dot_general(
        left, right, (((1,), (1,)), ((), ())), preferred_element_type=jnp.float32
    )


def per_device(inputs, up_weight, down_weight, out_grad):
    tokens = ("ia", "ka")
    token_in = lax.all_gather(inputs, tokens, axis=0, tiled=True)
    grad_in = lax.all_gather(out_grad, tokens, axis=0, tiled=True)

    def forward(rows):
        part = jnp.dot(token_in[rows], up_weight, preferred_element_type=jnp.float32)
        grad = contract_cols(grad_in[rows], down_weight)
        preact = lax.psum_scatter(
            part.astype(jnp.bfloat16), "ja", scatter_dimension=0, tiled=True
        ).astype(jnp.float32)
        hidden_grad = lax.psum_scatter(
            grad.astype(jnp.bfloat16), "ja", scatter_dimension=0, tiled=True
        ).astype(jnp.float32)
        hidden = gelu_value(preact).astype(jnp.bfloat16)
        preact_grad = (hidden_grad * gelu_slope(preact)).astype(jnp.bfloat16)
        return (
            lax.all_gather(hidden, "ja", axis=0, tiled=True),
            lax.all_gather(preact_grad, "ja", axis=0, tiled=True),
        )

    step = token_in.shape[0] // CHUNKS
    pieces = [forward(slice(c * step, (c + 1) * step)) for c in range(CHUNKS)]
    hidden = jnp.concatenate([piece[0] for piece in pieces], axis=0)
    preact_grad = jnp.concatenate([piece[1] for piece in pieces], axis=0)
    output = lax.psum_scatter(
        jnp.dot(hidden, down_weight, preferred_element_type=jnp.float32).astype(jnp.bfloat16),
        tokens, scatter_dimension=0, tiled=True,
    )
    input_grad = lax.psum_scatter(
        contract_cols(preact_grad, up_weight).astype(jnp.bfloat16),
        tokens, scatter_dimension=0, tiled=True,
    )
    up_grad = contract_rows(token_in, preact_grad).astype(jnp.bfloat16)
    down_grad = contract_rows(hidden, grad_in).astype(jnp.bfloat16)
    return (output, input_grad, up_grad, down_grad)


def solution(mesh):
    placed = (
        P(("ia", "ka"), "ja"),
        P("ja", ("ka", "ia")),
        P(("ka", "ia"), "ja"),
        P(("ia", "ka"), "ja"),
    )
    return jax.shard_map(
        per_device,
        mesh=mesh,
        in_specs=placed,
        out_specs=(
            P(("ia", "ka"), "ja"),
            P(("ia", "ka"), "ja"),
            P("ja", ("ka", "ia")),
            P(("ka", "ia"), "ja"),
        ),
        check_vma=False,
    )
```

```python
import functools

import jax
import jax.numpy as jnp
from jax import lax
from jax.experimental import pallas as pl
from jax.experimental.pallas import tpu as pltpu
from jax.sharding import PartitionSpec as P

sqrt_two_over_pi = 0.7978845608028654
cubic_coeff = 0.044715

MESH = pl.DeviceIdType.MESH
BF16 = jnp.bfloat16
F32 = jnp.float32

CHUNKS = 8
SLOTS = 4
WIDE = 1024

NAMES = (
    "tok_y", "tok_z_up", "tok_z_down", "tok_z0", "tok_z1", "tok_core",
    "a_t0", "a_t1", "a_d0", "a_d1", "a_s0", "a_s1", "a_y",
    "b_t0", "b_t1", "b_d0", "b_d1", "b_s0", "b_s1", "b_y",
    "ga_y", "ga_up", "ga_down", "ga_x0", "ga_x1",
    "gb_y", "gb_up", "gb_down", "gb_x0", "gb_x1",
    "o_core", "o_t0", "o_t1", "o_d0", "o_d1", "o_s0", "o_s1", "o_y",
)
INDEX = {name: place for place, name in enumerate(NAMES)}


def gelu_pair(preact):
    tanh_inner = jnp.tanh(sqrt_two_over_pi * (preact + cubic_coeff * preact * preact * preact))
    inner_slope = sqrt_two_over_pi * (1.0 + 3.0 * cubic_coeff * preact * preact)
    value = 0.5 * preact * (1.0 + tanh_inner)
    slope = 0.5 * (1.0 + tanh_inner) + 0.5 * preact * (1.0 - tanh_inner * tanh_inner) * inner_slope
    return value, slope


def contract(left, right, dims):
    return lax.dot_general(left, right, (dims, ((), ())), preferred_element_type=F32)


def kernel(
    x_ref, u_ref, w_ref, g_ref, out_ref, ing_ref, du_ref, dw_ref,
    tok, pa, pb, ta, da, sa, ya_out, ya_in, ya_own, rb, tb, db, sb, ha, hb,
    part, cr, tz, dz, sz, yo_out, yo_in, yo_own, acc_u, acc_w, send_sem, recv_sem,
):
    z0 = lax.axis_index("ia")
    ja = lax.axis_index("ja")
    ka = lax.axis_index("ka")
    y0, x0 = ja // 4, ja % 4
    h0, c0 = ka // 2, ka % 2
    rows = x_ref.shape[0] // CHUNKS

    def at_x(step):
        return (z0, y0 * 4 + (x0 + step + 4) % 4, ka)

    def at_z(step):
        return ((z0 + step + 4) % 4, ja, ka)

    y_pair = (z0, (1 - y0) * 4 + x0, ka)
    h_pair = (z0, ja, (1 - h0) * 2 + c0)
    c_pair = (z0, ja, h0 * 2 + 1 - c0)
    ways = ((0, 1), (1, -1))

    barrier = pltpu.get_barrier_semaphore()
    for other in (at_x(1), at_x(-1), at_z(1), at_z(-1), y_pair, h_pair, c_pair):
        pl.semaphore_signal(barrier, inc=1, device_id=other, device_id_type=MESH)
    for c in range(CHUNKS):
        tok[0, c, c0, z0, h0] = x_ref[c * rows:(c + 1) * rows]
        tok[1, c, c0, z0, h0] = g_ref[c * rows:(c + 1) * rows]
    acc_u[...] = jnp.zeros_like(acc_u)
    acc_w[...] = jnp.zeros_like(acc_w)
    pl.semaphore_wait(barrier, 7)

    def copy(name, c, src, dst, to):
        return pltpu.make_async_remote_copy(
            src_ref=src, dst_ref=dst,
            send_sem=send_sem.at[INDEX[name], c], recv_sem=recv_sem.at[INDEX[name], c],
            device_id=to, device_id_type=MESH,
        )

    def gather_first(name, c, ref_of, mine, to):
        return (
            copy(name + "_up", c, ref_of(mine), ref_of(mine), to(1)),
            copy(name + "_down", c, ref_of(mine), ref_of(mine), to(-1)),
        )

    def gather_second(name, c, ref_of, mine, to, axis):
        return tuple(
            copy(name + "_" + axis + str(t), c, ref_of(t, (mine - way + 4) % 4),
                 ref_of(t, (mine - way + 4) % 4), to(way))
            for t, way in ways
        )

    def sum_far(name, c, t, way, piece, transit, mine, to):
        return copy(f"{name}_t{t}", c, piece(t, (mine + 2) % 4), transit.at[t], to(way))

    def sum_near(name, c, t, way, piece, direct, mine, to):
        return copy(f"{name}_d{t}", c, piece(t, (mine - way + 4) % 4), direct.at[t], to(-way))

    def sum_first(name, c, t, way, piece, transit, direct, mine, to):
        return (
            sum_far(name, c, t, way, piece, transit, mine, to),
            sum_near(name, c, t, way, piece, direct, mine, to),
        )

    def sum_second(name, c, t, way, transit, second, to):
        return copy(f"{name}_s{t}", c, transit.at[t], second.at[t], to(way))

    def sum_middle(name, c, piece, transit, direct, second, mine, to):
        for t, way in ways:
            sum_far(name, c, t, way, piece, transit, mine, to).wait_recv()
            transit[t] = (transit[t].astype(F32) + piece(t, (mine + way + 4) % 4)[...].astype(F32)).astype(BF16)
            sum_second(name, c, t, way, transit, second, to).start()

    def sum_last(name, c, piece, transit, direct, second, mine, to):
        totals = []
        for t, way in ways:
            first, straight = sum_first(name, c, t, way, piece, transit, direct, mine, to)
            straight.wait_recv()
            last = sum_second(name, c, t, way, transit, second, to)
            last.wait_recv()
            first.wait_send()
            straight.wait_send()
            last.wait_send()
            totals.append(
                piece(t, mine)[...].astype(F32) + direct[t].astype(F32) + second[t].astype(F32)
            )
        return totals

    def tok_y(c):
        here = tok.at[:, c, c0, z0, h0]
        return copy("tok_y", c, here, here, h_pair)

    def tok_z(c, z):
        return tok.at[:, c, c0, z]

    def tok_z_one(c, t, z):
        return tok.at[t, c, c0, z]

    def tok_core(c):
        here = tok.at[:, c, c0]
        return copy("tok_core", c, here, here, c_pair)

    def a_piece(c, t, x):
        return pa.at[c % SLOTS, t, x]

    def a_args(c):
        s = c % SLOTS
        return functools.partial(a_piece, c), ta.at[s], da.at[s], sa.at[s], x0, at_x

    def a_y(c):
        s = c % SLOTS
        return copy("a_y", c, ya_out.at[s], ya_in.at[s], y_pair)

    def b_y(c):
        s = c % SLOTS
        return copy("b_y", c, pb.at[s, :, 1 - y0], rb.at[s], y_pair)

    def b_piece(c, t, x):
        return rb.at[c % SLOTS, t, x]

    def b_args(c):
        s = c % SLOTS
        return functools.partial(b_piece, c), tb.at[s], db.at[s], sb.at[s], x0, at_x

    def ga_y(c):
        here = ha.at[:, c, x0, y0]
        return copy("ga_y", c, here, here, y_pair)

    def gb_y(c):
        here = hb.at[:, c, y0]
        return copy("gb_y", c, here, here, y_pair)

    def ga_first(c):
        return gather_first("ga", c, lambda x: ha.at[:, c, x], x0, at_x)

    def ga_second(c):
        return gather_second("ga", c, lambda t, x: ha.at[t, c, x], x0, at_x, "x")

    def gb_first(c):
        return gather_first("gb", c, lambda x: hb.at[:, c, y0, x], x0, at_x)

    def gb_second(c):
        return gather_second("gb", c, lambda t, x: hb.at[t, c, y0, x], x0, at_x, "x")

    def tok_first(c):
        return gather_first("tok_z", c, functools.partial(tok_z, c), z0, at_z)

    def tok_second(c):
        return gather_second("tok", c, functools.partial(tok_z_one, c), z0, at_z, "z")

    def o_core(c):
        return copy("o_core", c, part.at[c % SLOTS, :, 1 - c0], cr.at[c], c_pair)

    def o_args(c):
        return (lambda t, z: cr.at[c, t, z]), tz.at[c], dz.at[c], sz.at[c], z0, at_z

    def o_y(c):
        return copy("o_y", c, yo_out.at[c % SLOTS], yo_in.at[c], h_pair)

    def start(copies):
        for one in copies:
            one.start()

    def finish(copies):
        for one in copies:
            one.wait_recv()
        for one in copies:
            one.wait_send()

    def wide(c, t):
        return tok[t, c].reshape(-1, tok.shape[-1])

    def gather_tokens_first(c):
        finish((tok_y(c),))
        start(tok_first(c))

    def gather_tokens_second(c):
        finish(tok_first(c))
        start(tok_second(c))

    def gather_tokens_core(c):
        finish(tok_second(c))
        start((tok_core(c),))

    def multiply_in(c):
        finish((tok_core(c),))
        s = c % SLOTS
        for t, way in ways:
            if t == 0:
                both = contract(wide(c, 0), u_ref[...], ((1,), (0,)))
            else:
                both = contract(wide(c, 1), w_ref[...], ((1,), (1,)))
            both = both.astype(BF16)
            pa[s, t] = both[:, :WIDE].reshape(pa.shape[2:])
            pb[s, t] = both[:, WIDE:].reshape(pb.shape[2:])
            piece, transit, direct, _, mine, to = a_args(c)
            start(sum_first("a", c, t, way, piece, transit, direct, mine, to))
        b_y(c).start()

    def sum_one(c):
        sum_middle("a", c, *a_args(c))
        b_y(c).wait_recv()
        s = c % SLOTS
        rb[s] = (rb[s].astype(F32) + pb[s, :, y0].astype(F32)).astype(BF16)
        piece, transit, direct, _, mine, to = b_args(c)
        for t, way in ways:
            start(sum_first("b", c, t, way, piece, transit, direct, mine, to))
        b_y(c).wait_send()

    def sum_two(c):
        s = c % SLOTS
        totals = sum_last("a", c, *a_args(c))
        for t in range(2):
            first, second = totals[t][0], totals[t][1]
            ya_own[s, t] = jnp.where(y0 == 0, first, second)
            ya_out[s, t] = jnp.where(y0 == 0, second, first).astype(BF16)
        a_y(c).start()
        sum_middle("b", c, *b_args(c))

    def activate(c):
        s = c % SLOTS
        finish((a_y(c),))
        value, slope = gelu_pair(ya_own[s, 0] + ya_in[s, 0].astype(F32))
        ha[0, c, x0, y0] = value.astype(BF16)
        ha[1, c, x0, y0] = ((ya_own[s, 1] + ya_in[s, 1].astype(F32)) * slope).astype(BF16)
        ga_y(c).start()
        totals = sum_last("b", c, *b_args(c))
        value, slope = gelu_pair(totals[0])
        hb[0, c, y0, x0] = value.astype(BF16)
        hb[1, c, y0, x0] = (totals[1] * slope).astype(BF16)
        start(gb_first(c))

    def gather_one(c):
        finish((ga_y(c),))
        start(ga_first(c))
        finish(gb_first(c))
        start(gb_second(c))

    def gather_two(c):
        finish(ga_first(c))
        start(ga_second(c))
        finish(gb_second(c))
        start((gb_y(c),))

    def multiply_out(c):
        finish(ga_second(c))
        finish((gb_y(c),))
        s = c % SLOTS
        for t in range(2):
            left_a = ha[t, c].reshape(-1, ha.shape[-1])
            left_b = hb[t, c].reshape(-1, hb.shape[-1])
            if t == 0:
                both = contract(left_a, w_ref[:WIDE], ((1,), (0,)))
                both += contract(left_b, w_ref[WIDE:], ((1,), (0,)))
            else:
                both = contract(left_a, u_ref[:, :WIDE], ((1,), (1,)))
                both += contract(left_b, u_ref[:, WIDE:], ((1,), (1,)))
            part[s, t] = both.astype(BF16).reshape(part.shape[2:])
        o_core(c).start()
        for cols, src in ((slice(None, WIDE), ha), (slice(WIDE, None), hb)):
            acc_u[:, cols] += contract(wide(c, 0), src[1, c].reshape(-1, src.shape[-1]), ((0,), (0,)))
            acc_w[cols] += contract(src[0, c].reshape(-1, src.shape[-1]), wide(c, 1), ((0,), (0,)))

    def total_one(c):
        finish((o_core(c),))
        s = c % SLOTS
        cr[c] = (cr[c].astype(F32) + part[s, :, c0].astype(F32)).astype(BF16)
        piece, transit, direct, _, mine, to = o_args(c)
        for t, way in ways:
            start(sum_first("o", c, t, way, piece, transit, direct, mine, to))

    def total_two(c):
        sum_middle("o", c, *o_args(c))

    def total_three(c):
        s = c % SLOTS
        totals = sum_last("o", c, *o_args(c))
        for t in range(2):
            first, second = totals[t][0], totals[t][1]
            yo_own[s, t] = jnp.where(h0 == 0, first, second)
            yo_out[s, t] = jnp.where(h0 == 0, second, first).astype(BF16)
        o_y(c).start()

    def total_four(c):
        s = c % SLOTS
        finish((o_y(c),))
        at = pl.ds(pl.multiple_of(c * rows, rows), rows)
        out_ref[at, :] = (yo_own[s, 0] + yo_in[c, 0].astype(F32)).astype(BF16)
        ing_ref[at, :] = (yo_own[s, 1] + yo_in[c, 1].astype(F32)).astype(BF16)

    stages = (
        gather_tokens_first, gather_tokens_second, gather_tokens_core, multiply_in,
        sum_one, sum_two, activate, gather_one, gather_two, multiply_out,
        total_one, total_two, total_three, total_four,
    )

    for c in range(CHUNKS):
        tok_y(c).start()

    def step(number, carry):
        for behind, stage in reversed(tuple(enumerate(stages))):
            @pl.when((number >= behind) & (number < behind + CHUNKS))
            def _():
                stage(number - behind)
        return carry

    lax.fori_loop(0, CHUNKS + len(stages) - 1, step, 0)
    du_ref[...] = acc_u[...].astype(BF16)
    dw_ref[...] = acc_w[...].astype(BF16)


def per_device(inputs, up_weight, down_weight, out_grad):
    tokens, width = inputs.shape
    hidden = up_weight.shape[1]
    rows = tokens // CHUNKS
    owned = rows * 2
    narrow = hidden - WIDE

    def vmem(*shape, dtype=BF16):
        return pltpu.VMEM(shape, dtype)

    scratch = [
        vmem(2, CHUNKS, 2, 4, 2, rows, width),
        vmem(SLOTS, 2, 4, 2, owned, WIDE),
        vmem(SLOTS, 2, 2, 4, owned, narrow),
        *[vmem(SLOTS, 2, 2, owned, WIDE)] * 3,
        vmem(SLOTS, 2, owned, WIDE),
        vmem(SLOTS, 2, owned, WIDE),
        vmem(SLOTS, 2, owned, WIDE, dtype=F32),
        vmem(SLOTS, 2, 4, owned, narrow),
        *[vmem(SLOTS, 2, owned, narrow)] * 3,
        vmem(2, CHUNKS, 4, 2, owned, WIDE),
        vmem(2, CHUNKS, 2, 4, owned, narrow),
        vmem(SLOTS, 2, 2, 4, 2, rows, width),
        vmem(CHUNKS, 2, 4, 2, rows, width),
        *[vmem(CHUNKS, 2, 2, rows, width)] * 3,
        vmem(SLOTS, 2, rows, width),
        vmem(CHUNKS, 2, rows, width),
        vmem(SLOTS, 2, rows, width, dtype=F32),
        vmem(width, hidden, dtype=F32),
        vmem(hidden, width, dtype=F32),
        pltpu.SemaphoreType.DMA((len(NAMES), CHUNKS)),
        pltpu.SemaphoreType.DMA((len(NAMES), CHUNKS)),
    ]
    return pl.pallas_call(
        kernel,
        out_shape=(
            jax.ShapeDtypeStruct(inputs.shape, BF16),
            jax.ShapeDtypeStruct(inputs.shape, BF16),
            jax.ShapeDtypeStruct(up_weight.shape, BF16),
            jax.ShapeDtypeStruct(down_weight.shape, BF16),
        ),
        in_specs=[pl.BlockSpec(memory_space=pltpu.VMEM)] * 4,
        out_specs=[pl.BlockSpec(memory_space=pltpu.VMEM)] * 4,
        scratch_shapes=scratch,
        compiler_params=pltpu.CompilerParams(
            collective_id=0, has_side_effects=True, vmem_limit_bytes=62 * 1024 * 1024
        ),
    )(inputs, up_weight, down_weight, out_grad)


def solution(mesh):
    placed = (
        P(("ia", "ka"), "ja"),
        P("ja", ("ka", "ia")),
        P(("ka", "ia"), "ja"),
        P(("ia", "ka"), "ja"),
    )
    return jax.shard_map(
        per_device,
        mesh=mesh,
        in_specs=placed,
        out_specs=(
            P(("ia", "ka"), "ja"),
            P(("ia", "ka"), "ja"),
            P("ja", ("ka", "ia")),
            P(("ka", "ia"), "ja"),
        ),
        check_vma=False,
    )
```

```python
import functools

import jax
import jax.numpy as jnp
from jax import lax
from jax.experimental import pallas as pl
from jax.experimental.pallas import tpu as pltpu
from jax.sharding import PartitionSpec as P

sqrt_two_over_pi = 0.7978845608028654
cubic_coeff = 0.044715

MESH = pl.DeviceIdType.MESH
BF16 = jnp.bfloat16
F32 = jnp.float32

CHUNKS = 8
SLOTS = 4
WIDE = 896

NAMES = (
    "tok_y", "tok_z_up", "tok_z_down", "tok_z0", "tok_z1", "tok_core",
    "a_t0", "a_t1", "a_d0", "a_d1", "a_s0", "a_s1", "a_y",
    "b_t0", "b_t1", "b_d0", "b_d1", "b_s0", "b_s1", "b_y",
    "ga_y", "ga_up", "ga_down", "ga_x0", "ga_x1",
    "gb_y", "gb_up", "gb_down", "gb_x0", "gb_x1",
    "o_core", "o_t0", "o_t1", "o_d0", "o_d1", "o_s0", "o_s1", "o_y",
)
INDEX = {name: place for place, name in enumerate(NAMES)}


def gelu_pair(preact):
    tanh_inner = jnp.tanh(sqrt_two_over_pi * (preact + cubic_coeff * preact * preact * preact))
    inner_slope = sqrt_two_over_pi * (1.0 + 3.0 * cubic_coeff * preact * preact)
    value = 0.5 * preact * (1.0 + tanh_inner)
    slope = 0.5 * (1.0 + tanh_inner) + 0.5 * preact * (1.0 - tanh_inner * tanh_inner) * inner_slope
    return value, slope


def contract(left, right, dims):
    return lax.dot_general(left, right, (dims, ((), ())), preferred_element_type=F32)


def kernel(
    x_ref, u_hbm, w_hbm, g_ref, out_ref, ing_ref, du_hbm, dw_hbm,
    u_ref, w_ref, du_ref, dw_ref, local_sem,
    tok, pa, pb, ta, da, sa, ya_out, ya_in, ya_own, rb, tb, db, sb, ha, hb,
    part, cr, tz, dz, sz, yo_out, yo_in, yo_own, acc_u, acc_w, send_sem, recv_sem,
):
    z0 = lax.axis_index("ia")
    ja = lax.axis_index("ja")
    ka = lax.axis_index("ka")
    y0, x0 = ja // 4, ja % 4
    h0, c0 = ka // 2, ka % 2
    rows = x_ref.shape[0] // CHUNKS

    def at_x(step):
        return (z0, y0 * 4 + (x0 + step + 4) % 4, ka)

    def at_z(step):
        return ((z0 + step + 4) % 4, ja, ka)

    y_pair = (z0, (1 - y0) * 4 + x0, ka)
    h_pair = (z0, ja, (1 - h0) * 2 + c0)
    c_pair = (z0, ja, h0 * 2 + 1 - c0)
    ways = ((0, 1), (1, -1))

    load_u = pltpu.make_async_copy(u_hbm, u_ref, local_sem.at[0])
    load_w = pltpu.make_async_copy(w_hbm, w_ref, local_sem.at[1])
    store_u = pltpu.make_async_copy(du_ref, du_hbm, local_sem.at[2])
    store_w = pltpu.make_async_copy(dw_ref, dw_hbm, local_sem.at[3])
    load_u.start()
    load_w.start()

    barrier = pltpu.get_barrier_semaphore()
    for other in (at_x(1), at_x(-1), at_z(1), at_z(-1), y_pair, h_pair, c_pair):
        pl.semaphore_signal(barrier, inc=1, device_id=other, device_id_type=MESH)
    for c in range(CHUNKS):
        tok[0, c, c0, z0, h0] = x_ref[c * rows:(c + 1) * rows]
        tok[1, c, c0, z0, h0] = g_ref[c * rows:(c + 1) * rows]
    pl.semaphore_wait(barrier, 7)

    def copy(name, c, src, dst, to):
        return pltpu.make_async_remote_copy(
            src_ref=src, dst_ref=dst,
            send_sem=send_sem.at[INDEX[name], c], recv_sem=recv_sem.at[INDEX[name], c],
            device_id=to, device_id_type=MESH,
        )

    def gather_first(name, c, ref_of, mine, to):
        return (
            copy(name + "_up", c, ref_of(mine), ref_of(mine), to(1)),
            copy(name + "_down", c, ref_of(mine), ref_of(mine), to(-1)),
        )

    def gather_second(name, c, ref_of, mine, to, axis):
        return tuple(
            copy(name + "_" + axis + str(t), c, ref_of(t, (mine - way + 4) % 4),
                 ref_of(t, (mine - way + 4) % 4), to(way))
            for t, way in ways
        )

    def sum_far(name, c, t, way, piece, transit, mine, to):
        return copy(f"{name}_t{t}", c, piece(t, (mine + 2) % 4), transit.at[t], to(way))

    def sum_near(name, c, t, way, piece, direct, mine, to):
        return copy(f"{name}_d{t}", c, piece(t, (mine - way + 4) % 4), direct.at[t], to(-way))

    def sum_first(name, c, t, way, piece, transit, direct, mine, to):
        return (
            sum_far(name, c, t, way, piece, transit, mine, to),
            sum_near(name, c, t, way, piece, direct, mine, to),
        )

    def sum_second(name, c, t, way, transit, second, to):
        return copy(f"{name}_s{t}", c, transit.at[t], second.at[t], to(way))

    def sum_middle(name, c, piece, transit, direct, second, mine, to):
        for t, way in ways:
            sum_far(name, c, t, way, piece, transit, mine, to).wait_recv()
            transit[t] = (transit[t].astype(F32) + piece(t, (mine + way + 4) % 4)[...].astype(F32)).astype(BF16)
            sum_second(name, c, t, way, transit, second, to).start()

    def sum_last(name, c, piece, transit, direct, second, mine, to):
        totals = []
        for t, way in ways:
            first, straight = sum_first(name, c, t, way, piece, transit, direct, mine, to)
            straight.wait_recv()
            last = sum_second(name, c, t, way, transit, second, to)
            last.wait_recv()
            first.wait_send()
            straight.wait_send()
            last.wait_send()
            totals.append(
                piece(t, mine)[...].astype(F32) + direct[t].astype(F32) + second[t].astype(F32)
            )
        return totals

    def tok_y(c):
        here = tok.at[:, c, c0, z0, h0]
        return copy("tok_y", c, here, here, h_pair)

    def tok_z(c, z):
        return tok.at[:, c, c0, z]

    def tok_z_one(c, t, z):
        return tok.at[t, c, c0, z]

    def tok_core(c):
        here = tok.at[:, c, c0]
        return copy("tok_core", c, here, here, c_pair)

    def a_piece(c, t, x):
        return pa.at[c % SLOTS, t, x]

    def a_args(c):
        s = c % SLOTS
        return functools.partial(a_piece, c), ta.at[s], da.at[s], sa.at[s], x0, at_x

    def a_y(c):
        s = c % SLOTS
        return copy("a_y", c, ya_out.at[s], ya_in.at[s], y_pair)

    def b_y(c):
        s = c % SLOTS
        return copy("b_y", c, pb.at[s, :, 1 - y0], rb.at[s], y_pair)

    def b_piece(c, t, x):
        return rb.at[c % SLOTS, t, x]

    def b_args(c):
        s = c % SLOTS
        return functools.partial(b_piece, c), tb.at[s], db.at[s], sb.at[s], x0, at_x

    def ga_y(c):
        here = ha.at[:, c, x0, y0]
        return copy("ga_y", c, here, here, y_pair)

    def gb_y(c):
        here = hb.at[:, c, y0]
        return copy("gb_y", c, here, here, y_pair)

    def ga_first(c):
        return gather_first("ga", c, lambda x: ha.at[:, c, x], x0, at_x)

    def ga_second(c):
        return gather_second("ga", c, lambda t, x: ha.at[t, c, x], x0, at_x, "x")

    def gb_first(c):
        return gather_first("gb", c, lambda x: hb.at[:, c, y0, x], x0, at_x)

    def gb_second(c):
        return gather_second("gb", c, lambda t, x: hb.at[t, c, y0, x], x0, at_x, "x")

    def tok_first(c):
        return gather_first("tok_z", c, functools.partial(tok_z, c), z0, at_z)

    def tok_second(c):
        return gather_second("tok", c, functools.partial(tok_z_one, c), z0, at_z, "z")

    def o_core(c):
        return copy("o_core", c, part.at[c % SLOTS, :, 1 - c0], cr.at[c], c_pair)

    def o_args(c):
        return (lambda t, z: cr.at[c, t, z]), tz.at[c], dz.at[c], sz.at[c], z0, at_z

    def o_y(c):
        return copy("o_y", c, yo_out.at[c % SLOTS], yo_in.at[c], h_pair)

    def start(copies):
        for one in copies:
            one.start()

    def finish(copies):
        for one in copies:
            one.wait_recv()
        for one in copies:
            one.wait_send()

    def wide(c, t):
        return tok[t, c].reshape(-1, tok.shape[-1])

    def gather_tokens_first(c):
        finish((tok_y(c),))
        start(tok_first(c))

    def gather_tokens_second(c):
        finish(tok_first(c))
        start(tok_second(c))

    def gather_tokens_core(c):
        finish(tok_second(c))
        start((tok_core(c),))

    def multiply_in(c):
        finish((tok_core(c),))
        s = c % SLOTS
        for t, way in ways:
            if t == 0:
                both = contract(wide(c, 0), u_ref[...], ((1,), (0,)))
            else:
                both = contract(wide(c, 1), w_ref[...], ((1,), (1,)))
            both = both.astype(BF16)
            pa[s, t] = both[:, :WIDE].reshape(pa.shape[2:])
            pb[s, t] = both[:, WIDE:].reshape(pb.shape[2:])
            piece, transit, direct, _, mine, to = a_args(c)
            start(sum_first("a", c, t, way, piece, transit, direct, mine, to))
        b_y(c).start()

    def sum_one(c):
        sum_middle("a", c, *a_args(c))
        b_y(c).wait_recv()
        s = c % SLOTS
        rb[s] = (rb[s].astype(F32) + pb[s, :, y0].astype(F32)).astype(BF16)
        piece, transit, direct, _, mine, to = b_args(c)
        for t, way in ways:
            start(sum_first("b", c, t, way, piece, transit, direct, mine, to))
        b_y(c).wait_send()

    def sum_two(c):
        s = c % SLOTS
        totals = sum_last("a", c, *a_args(c))
        for t in range(2):
            first, second = totals[t][0], totals[t][1]
            ya_own[s, t] = jnp.where(y0 == 0, first, second)
            ya_out[s, t] = jnp.where(y0 == 0, second, first).astype(BF16)
        a_y(c).start()
        sum_middle("b", c, *b_args(c))

    def activate(c):
        s = c % SLOTS
        finish((a_y(c),))
        value, slope = gelu_pair(ya_own[s, 0] + ya_in[s, 0].astype(F32))
        ha[0, c, x0, y0] = value.astype(BF16)
        ha[1, c, x0, y0] = ((ya_own[s, 1] + ya_in[s, 1].astype(F32)) * slope).astype(BF16)
        ga_y(c).start()
        totals = sum_last("b", c, *b_args(c))
        value, slope = gelu_pair(totals[0])
        hb[0, c, y0, x0] = value.astype(BF16)
        hb[1, c, y0, x0] = (totals[1] * slope).astype(BF16)
        start(gb_first(c))

    def gather_one(c):
        finish((ga_y(c),))
        start(ga_first(c))
        finish(gb_first(c))
        start(gb_second(c))

    def gather_two(c):
        finish(ga_first(c))
        start(ga_second(c))
        finish(gb_second(c))
        start((gb_y(c),))

    def multiply_out(c):
        finish(ga_second(c))
        finish((gb_y(c),))
        s = c % SLOTS
        for t in range(2):
            left_a = ha[t, c].reshape(-1, ha.shape[-1])
            left_b = hb[t, c].reshape(-1, hb.shape[-1])
            if t == 0:
                both = contract(left_a, w_ref[:WIDE], ((1,), (0,)))
                both += contract(left_b, w_ref[WIDE:], ((1,), (0,)))
            else:
                both = contract(left_a, u_ref[:, :WIDE], ((1,), (1,)))
                both += contract(left_b, u_ref[:, WIDE:], ((1,), (1,)))
            part[s, t] = both.astype(BF16).reshape(part.shape[2:])
        o_core(c).start()

    def add_grads(c):
        for cols, src in ((slice(None, WIDE), ha), (slice(WIDE, None), hb)):
            acc_u[:, cols] += contract(wide(c, 0), src[1, c].reshape(-1, src.shape[-1]), ((0,), (0,)))
            acc_w[cols] += contract(src[0, c].reshape(-1, src.shape[-1]), wide(c, 1), ((0,), (0,)))

    def total_one(c):
        finish((o_core(c),))
        s = c % SLOTS
        cr[c] = (cr[c].astype(F32) + part[s, :, c0].astype(F32)).astype(BF16)
        piece, transit, direct, _, mine, to = o_args(c)
        for t, way in ways:
            start(sum_first("o", c, t, way, piece, transit, direct, mine, to))
        add_grads(c)

    def total_two(c):
        sum_middle("o", c, *o_args(c))

        @pl.when(c == CHUNKS - 1)
        def _():
            du_ref[...] = acc_u[...].astype(BF16)
            store_u.start()
            dw_ref[...] = acc_w[...].astype(BF16)
            store_w.start()

    def total_three(c):
        s = c % SLOTS
        totals = sum_last("o", c, *o_args(c))
        for t in range(2):
            first, second = totals[t][0], totals[t][1]
            yo_own[s, t] = jnp.where(h0 == 0, first, second)
            yo_out[s, t] = jnp.where(h0 == 0, second, first).astype(BF16)
        o_y(c).start()

    def total_four(c):
        s = c % SLOTS
        finish((o_y(c),))
        at = pl.ds(pl.multiple_of(c * rows, rows), rows)
        out_ref[at, :] = (yo_own[s, 0] + yo_in[c, 0].astype(F32)).astype(BF16)
        ing_ref[at, :] = (yo_own[s, 1] + yo_in[c, 1].astype(F32)).astype(BF16)

    stages = (
        gather_tokens_first, gather_tokens_second, gather_tokens_core, multiply_in,
        sum_one, sum_two, activate, gather_one, gather_two, multiply_out,
        total_one, total_two, total_three, total_four,
    )

    for c in range(CHUNKS):
        tok_y(c).start()
    acc_u[...] = jnp.zeros_like(acc_u)
    acc_w[...] = jnp.zeros_like(acc_w)
    load_u.wait()
    load_w.wait()

    def step(number, carry):
        for behind, stage in reversed(tuple(enumerate(stages))):
            @pl.when((number >= behind) & (number < behind + CHUNKS))
            def _():
                stage(number - behind)
        return carry

    lax.fori_loop(0, CHUNKS + len(stages) - 1, step, 0)
    store_u.wait()
    store_w.wait()


def hand_on(*refs):
    sources, targets, held, sem = refs[:4], refs[4:8], refs[8:12], refs[12]
    copies = []
    for source, target, room in zip(sources, targets, held):
        parts = max(1, source.shape[0] // 384)
        rows = source.shape[0] // parts
        for number in range(parts):
            at = pl.ds(number * rows, rows)
            place = len(copies)
            copies.append((
                pltpu.make_async_copy(source.at[at], room.at[at], sem.at[0, place]),
                pltpu.make_async_copy(room.at[at], target.at[at], sem.at[1, place]),
            ))
    for load, _ in copies:
        load.start()
    for load, store in copies:
        load.wait()
        store.start()
    for _, store in copies:
        store.wait()


def per_device(inputs, up_weight, down_weight, out_grad):
    tokens, width = inputs.shape
    hidden = up_weight.shape[1]
    rows = tokens // CHUNKS
    owned = rows * 2
    narrow = hidden - WIDE

    def vmem(*shape, dtype=BF16):
        return pltpu.VMEM(shape, dtype)

    scratch = [
        vmem(width, hidden),
        vmem(hidden, width),
        vmem(width, hidden),
        vmem(hidden, width),
        pltpu.SemaphoreType.DMA((4,)),
        vmem(2, CHUNKS, 2, 4, 2, rows, width),
        vmem(SLOTS, 2, 4, 2, owned, WIDE),
        vmem(SLOTS, 2, 2, 4, owned, narrow),
        *[vmem(SLOTS, 2, 2, owned, WIDE)] * 3,
        vmem(SLOTS, 2, owned, WIDE),
        vmem(SLOTS, 2, owned, WIDE),
        vmem(SLOTS, 2, owned, WIDE, dtype=F32),
        vmem(SLOTS, 2, 4, owned, narrow),
        *[vmem(SLOTS, 2, owned, narrow)] * 3,
        vmem(2, CHUNKS, 4, 2, owned, WIDE),
        vmem(2, CHUNKS, 2, 4, owned, narrow),
        vmem(SLOTS, 2, 2, 4, 2, rows, width),
        vmem(CHUNKS, 2, 4, 2, rows, width),
        *[vmem(CHUNKS, 2, 2, rows, width)] * 3,
        vmem(SLOTS, 2, rows, width),
        vmem(CHUNKS, 2, rows, width),
        vmem(SLOTS, 2, rows, width, dtype=F32),
        vmem(width, hidden, dtype=F32),
        vmem(hidden, width, dtype=F32),
        pltpu.SemaphoreType.DMA((len(NAMES), CHUNKS)),
        pltpu.SemaphoreType.DMA((len(NAMES), CHUNKS)),
    ]
    results = (
        jax.ShapeDtypeStruct(inputs.shape, BF16),
        jax.ShapeDtypeStruct(inputs.shape, BF16),
        jax.ShapeDtypeStruct(up_weight.shape, BF16),
        jax.ShapeDtypeStruct(down_weight.shape, BF16),
    )
    near, far = pl.BlockSpec(memory_space=pltpu.VMEM), pl.BlockSpec(memory_space=pl.ANY)
    made = pl.pallas_call(
        kernel,
        out_shape=results,
        in_specs=[near, far, far, near],
        out_specs=[near, near, far, far],
        scratch_shapes=scratch,
        compiler_params=pltpu.CompilerParams(
            collective_id=0, has_side_effects=True, vmem_limit_bytes=62 * 1024 * 1024
        ),
    )(inputs, up_weight, down_weight, out_grad)
    return pl.pallas_call(
        hand_on,
        out_shape=results,
        in_specs=[far] * 4,
        out_specs=[far] * 4,
        scratch_shapes=[vmem(*one.shape) for one in results] + [pltpu.SemaphoreType.DMA((2, 8))],
        compiler_params=pltpu.CompilerParams(vmem_limit_bytes=62 * 1024 * 1024),
    )(*made)


def solution(mesh):
    placed = (
        P(("ia", "ka"), "ja"),
        P("ja", ("ka", "ia")),
        P(("ka", "ia"), "ja"),
        P(("ia", "ka"), "ja"),
    )
    return jax.shard_map(
        per_device,
        mesh=mesh,
        in_specs=placed,
        out_specs=(
            P(("ia", "ka"), "ja"),
            P(("ia", "ka"), "ja"),
            P("ja", ("ka", "ia")),
            P(("ka", "ia"), "ja"),
        ),
        check_vma=False,
    )
```

```python
import functools

import jax
import jax.numpy as jnp
from jax import lax
from jax.experimental import pallas as pl
from jax.experimental.pallas import tpu as pltpu
from jax.sharding import PartitionSpec as P

sqrt_two_over_pi = 0.7978845608028654
cubic_coeff = 0.044715

MESH = pl.DeviceIdType.MESH
BF16 = jnp.bfloat16
F32 = jnp.float32

CHUNKS = 8
SLOTS = 4
HELD = 3
WIDE = 896

RECEIVED = 3
SENT = 2
NAMES = (
    "tok_z1", "tok_z2", "tok_z3", "tok_core",
    "a_t0", "a_t1", "a_d0", "a_d1", "a_s0", "a_s1", "a_y",
    "b_t0", "b_t1", "b_d0", "b_d1", "b_s0", "b_s1", "b_y0", "b_y1",
    "ga_y", "ga_up", "ga_down", "ga_x0", "ga_x1", "gp_up", "gp_down", "gp_x0", "gp_x1",
    "gb_y0", "gb_y1", "gb_y2", "gb_y3", "gb_up", "gb_down", "gb_x0", "gb_x1",
    "o_core0", "o_core1", "o_z1", "o_z2", "o_z3", "o_y",
)
PEERS = tuple((step, turn) for step in range(4) for turn in range(2))[1:]
INDEX = {name: place for place, name in enumerate(NAMES)}


def gelu_pair(preact):
    tanh_inner = jnp.tanh(sqrt_two_over_pi * (preact + cubic_coeff * preact * preact * preact))
    inner_slope = sqrt_two_over_pi * (1.0 + 3.0 * cubic_coeff * preact * preact)
    value = 0.5 * preact * (1.0 + tanh_inner)
    slope = 0.5 * (1.0 + tanh_inner) + 0.5 * preact * (1.0 - tanh_inner * tanh_inner) * inner_slope
    return value, slope


def contract(left, right, dims):
    return lax.dot_general(left, right, (dims, ((), ())), preferred_element_type=F32)


def kernel(
    x_hbm, u_hbm, w_hbm, g_hbm, out_ref, ing_ref, du_hbm, dw_hbm,
    u_ref, w_ref, du_ref, dw_ref, local_sem,
    tok, pa, pb, ta, da, sa, ya_out, ya_in, ya_own, rb, tb, db, sb, ha, hb,
    part, cr, zr, last_in, yo_out, yo_in, yo_own, acc_u, acc_w, send_sem, recv_sem, peer_sem, tok_sem,
):
    z0 = lax.axis_index("ia")
    ja = lax.axis_index("ja")
    ka = lax.axis_index("ka")
    y0, x0 = ja // 4, ja % 4
    h0, c0 = ka // 2, ka % 2
    rows = x_hbm.shape[1]
    last = CHUNKS - 1

    def at_x(step):
        return (z0, y0 * 4 + (x0 + step + 4) % 4, ka)

    def at_z(step):
        return ((z0 + step + 4) % 4, ja, ka)

    y_pair = (z0, (1 - y0) * 4 + x0, ka)
    h_pair = (z0, ja, (1 - h0) * 2 + c0)
    c_pair = (z0, ja, h0 * 2 + 1 - c0)
    ways = ((0, 1), (1, -1))

    barrier = pltpu.get_barrier_semaphore()
    peers = [((z0 + step) % 4, ja, (h0 + turn) % 2 * 2 + c0) for step, turn in PEERS]
    for other in [at_x(1), at_x(-1), y_pair, c_pair] + peers:
        pl.semaphore_signal(barrier, inc=1, device_id=other, device_id_type=MESH)
    load_x = pltpu.make_async_copy(x_hbm, tok.at[0, :, c0, z0, h0], local_sem.at[4])
    load_g = pltpu.make_async_copy(g_hbm, tok.at[1, :, c0, z0, h0], local_sem.at[5])
    load_u = pltpu.make_async_copy(u_hbm, u_ref, local_sem.at[0])
    load_w = pltpu.make_async_copy(w_hbm, w_ref, local_sem.at[1])
    store_u = pltpu.make_async_copy(du_ref, du_hbm, local_sem.at[2])
    store_w = pltpu.make_async_copy(dw_ref, dw_hbm, local_sem.at[3])
    for one in (load_x, load_g, load_u, load_w):
        one.start()
    load_x.wait()
    load_g.wait()
    pl.semaphore_wait(barrier, 4 + len(PEERS))

    def copy(name, c, src, dst, to):
        return pltpu.make_async_remote_copy(
            src_ref=src, dst_ref=dst,
            send_sem=send_sem.at[INDEX[name], c % SENT], recv_sem=recv_sem.at[INDEX[name], c % RECEIVED],
            device_id=to, device_id_type=MESH,
        )

    def gather_first(name, c, ref_of, mine, to):
        return (
            copy(name + "_up", c, ref_of(mine), ref_of(mine), to(1)),
            copy(name + "_down", c, ref_of(mine), ref_of(mine), to(-1)),
        )

    def gather_second(name, c, ref_of, mine, to, axis):
        return tuple(
            copy(name + "_" + axis + str(t), c, ref_of(t, (mine - way + 4) % 4),
                 ref_of(t, (mine - way + 4) % 4), to(way))
            for t, way in ways
        )

    def sum_far(name, c, t, way, piece, transit, mine, to):
        return copy(f"{name}_t{t}", c, piece(t, (mine + 2) % 4), transit.at[t], to(way))

    def sum_near(name, c, t, way, piece, direct, mine, to):
        return copy(f"{name}_d{t}", c, piece(t, (mine - way + 4) % 4), direct.at[t], to(-way))

    def sum_first(name, c, t, way, piece, transit, direct, mine, to):
        return (
            sum_far(name, c, t, way, piece, transit, mine, to),
            sum_near(name, c, t, way, piece, direct, mine, to),
        )

    def sum_second(name, c, t, way, transit, second, to):
        return copy(f"{name}_s{t}", c, transit.at[t], second.at[t], to(way))

    def sum_middle(name, c, piece, transit, direct, second, mine, to):
        for t, way in ways:
            sum_far(name, c, t, way, piece, transit, mine, to).wait_recv()
            transit[t] = (transit[t].astype(F32) + piece(t, (mine + way + 4) % 4)[...].astype(F32)).astype(BF16)
            sum_second(name, c, t, way, transit, second, to).start()

    def sum_last(name, c, piece, transit, direct, second, mine, to):
        totals = []
        for t, way in ways:
            first, straight = sum_first(name, c, t, way, piece, transit, direct, mine, to)
            straight.wait_recv()
            last = sum_second(name, c, t, way, transit, second, to)
            last.wait_recv()
            first.wait_send()
            straight.wait_send()
            last.wait_send()
            totals.append(
                piece(t, mine)[...].astype(F32) + direct[t].astype(F32) + second[t].astype(F32)
            )
        return totals

    def tok_y(c):
        here = tok.at[:, c, c0, z0, h0]
        return pltpu.make_async_remote_copy(
            src_ref=here, dst_ref=here, send_sem=tok_sem.at[0, c], recv_sem=tok_sem.at[1, c],
            device_id=h_pair, device_id_type=MESH,
        )

    def tok_z(c):
        here = tok.at[:, c, c0, z0]
        return [copy(f"tok_z{step}", c, here, here, at_z(step)) for step in (1, 2, 3)]

    def peer_copy(which, place, src, dst):
        return pltpu.make_async_remote_copy(
            src_ref=src, dst_ref=dst,
            send_sem=peer_sem.at[which, 0, place], recv_sem=peer_sem.at[which, 1, place],
            device_id=peers[place], device_id_type=MESH,
        )

    def first_tokens():
        here = tok.at[:, 0, c0, z0, h0]
        return [peer_copy(0, place, here, here) for place in range(len(PEERS))]

    def last_sums():
        return [
            peer_copy(1, place, cr.at[last, :, (z0 + step) % 4, (h0 + turn) % 2], last_in.at[place])
            for place, (step, turn) in enumerate(PEERS)
        ]

    def tok_core(c):
        here = tok.at[:, c, c0]
        return copy("tok_core", c, here, here, c_pair)

    def a_piece(c, t, x):
        return pa.at[c % HELD, t, x]

    def a_args(c):
        s = c % SLOTS
        return functools.partial(a_piece, c), ta.at[s], da.at[s], sa.at[s], x0, at_x

    def a_y(c):
        s = c % SLOTS
        return copy("a_y", c, ya_out.at[s], ya_in.at[s], y_pair)

    def b_y(c, t):
        s = c % SLOTS
        return copy(f"b_y{t}", c, pb.at[c % HELD, t, 1 - y0], rb.at[s, t], y_pair)

    def b_piece(c, t, x):
        return rb.at[c % SLOTS, t, x]

    def b_args(c):
        s = c % SLOTS
        return functools.partial(b_piece, c), tb.at[s], db.at[s], sb.at[s], x0, at_x

    def ga_y(c):
        here = ha.at[:, c, x0, y0]
        return copy("ga_y", c, here, here, y_pair)

    def gb_y(c, step):
        here = hb.at[:, c, y0, (x0 + step) % 4]
        return copy(f"gb_y{step}", c, here, here, y_pair)

    def ga_first(c):
        return gather_first("ga", c, lambda x: ha.at[:, c, x, y0], x0, at_x)

    def ga_second(c):
        return gather_second("ga", c, lambda t, x: ha.at[t, c, x, y0], x0, at_x, "x")

    def gp_first(c):
        return gather_first("gp", c, lambda x: ha.at[:, c, x, 1 - y0], x0, at_x)

    def gp_second(c):
        return gather_second("gp", c, lambda t, x: ha.at[t, c, x, 1 - y0], x0, at_x, "x")

    def gb_first(c):
        return gather_first("gb", c, lambda x: hb.at[:, c, y0, x], x0, at_x)

    def gb_second(c):
        return gather_second("gb", c, lambda t, x: hb.at[t, c, y0, x], x0, at_x, "x")

    def o_core(c, t):
        return copy(f"o_core{t}", c, part.at[c % HELD, t, 1 - c0], cr.at[c, t], c_pair)

    def o_z(c):
        return [
            copy(f"o_z{step}", c, cr.at[c, :, (z0 + step) % 4], zr.at[c, step - 1], at_z(step))
            for step in (1, 2, 3)
        ]

    def o_y(c):
        return copy("o_y", c, yo_out.at[c % SLOTS], yo_in.at[c], h_pair)

    def start(copies):
        for one in copies:
            one.start()

    def finish(copies):
        for one in copies:
            one.wait_recv()
        for one in copies:
            one.wait_send()

    def wide(c, t):
        return tok[t, c].reshape(-1, tok.shape[-1])

    def gather_tokens(c):
        finish((tok_y(c),))
        start(tok_z(c))

    def gather_tokens_core(c):
        @pl.when(c > 0)
        def _():
            finish(tok_z(c))

        @pl.when(c == 0)
        def _():
            finish(first_tokens())

        start((tok_core(c),))

    def multiply_in(c):
        finish((tok_core(c),))
        s = c % HELD
        for t, way in ways:
            if t == 0:
                both = contract(wide(c, 0), u_ref[...], ((1,), (0,)))
            else:
                both = contract(wide(c, 1), w_ref[...], ((1,), (1,)))
            both = both.astype(BF16)
            pa[s, t] = both[:, :WIDE].reshape(pa.shape[2:])
            pb[s, t] = both[:, WIDE:].reshape(pb.shape[2:])
            piece, transit, direct, _, mine, to = a_args(c)
            b_y(c, t).start()
            start(sum_first("a", c, t, way, piece, transit, direct, mine, to))

    def sum_one(c):
        sum_middle("a", c, *a_args(c))
        s = c % SLOTS
        piece, transit, direct, _, mine, to = b_args(c)
        for t, way in ways:
            b_y(c, t).wait_recv()
            rb[s, t] = (rb[s, t].astype(F32) + pb[c % HELD, t, y0].astype(F32)).astype(BF16)
            start(sum_first("b", c, t, way, piece, transit, direct, mine, to))
        for t in range(2):
            b_y(c, t).wait_send()

    def sum_two(c):
        s = c % SLOTS
        totals = sum_last("a", c, *a_args(c))
        for t in range(2):
            first, second = totals[t][0], totals[t][1]
            ya_own[s, t] = jnp.where(y0 == 0, first, second)
            ya_out[s, t] = jnp.where(y0 == 0, second, first).astype(BF16)
        a_y(c).start()
        sum_middle("b", c, *b_args(c))

    def activate(c):
        s = c % SLOTS
        finish((a_y(c),))
        value, slope = gelu_pair(ya_own[s, 0] + ya_in[s, 0].astype(F32))
        ha[0, c, x0, y0] = value.astype(BF16)
        ha[1, c, x0, y0] = ((ya_own[s, 1] + ya_in[s, 1].astype(F32)) * slope).astype(BF16)
        ga_y(c).start()
        start(ga_first(c))
        totals = sum_last("b", c, *b_args(c))
        value, slope = gelu_pair(totals[0])
        hb[0, c, y0, x0] = value.astype(BF16)
        hb[1, c, y0, x0] = (totals[1] * slope).astype(BF16)
        gb_y(c, 0).start()
        start(gb_first(c))

    def gather_one(c):
        finish((ga_y(c),))
        start(gp_first(c))
        finish(gb_first(c))
        start(gb_second(c))
        start((gb_y(c, 1), gb_y(c, 3)))
        finish((gb_y(c, 0),))
        finish(ga_first(c))
        start(ga_second(c))

    def gather_two(c):
        finish(gp_first(c))
        start(gp_second(c))
        finish(gb_second(c))
        gb_y(c, 2).start()
        finish((gb_y(c, 1), gb_y(c, 3)))

    def multiply_out(c):
        finish(ga_second(c))
        finish(gp_second(c))
        finish((gb_y(c, 2),))
        s = c % HELD
        for t in range(2):
            left_a = ha[t, c].reshape(-1, ha.shape[-1])
            left_b = hb[t, c].reshape(-1, hb.shape[-1])
            if t == 0:
                both = contract(left_a, w_ref[:WIDE], ((1,), (0,)))
                both += contract(left_b, w_ref[WIDE:], ((1,), (0,)))
            else:
                both = contract(left_a, u_ref[:, :WIDE], ((1,), (1,)))
                both += contract(left_b, u_ref[:, WIDE:], ((1,), (1,)))
            part[s, t] = both.astype(BF16).reshape(part.shape[2:])
            o_core(c, t).start()

    def add_grads(c):
        for cols, src in ((slice(None, WIDE), ha), (slice(WIDE, None), hb)):
            acc_u[:, cols] += contract(wide(c, 0), src[1, c].reshape(-1, src.shape[-1]), ((0,), (0,)))
            acc_w[cols] += contract(src[0, c].reshape(-1, src.shape[-1]), wide(c, 1), ((0,), (0,)))

    def total_one(c):
        s = c % HELD
        for t in range(2):
            finish((o_core(c, t),))
            cr[c, t] = (cr[c, t].astype(F32) + part[s, t, c0].astype(F32)).astype(BF16)

        @pl.when(c < last)
        def _():
            start(o_z(c))

        @pl.when(c == last)
        def _():
            start(last_sums())

    def total_two(c):
        s = c % SLOTS

        @pl.when(c < last)
        def _():
            finish(o_z(c))
            for t in range(2):
                first, second = (
                    cr[c, t, z0, h].astype(F32) + zr[c, 0, t, h].astype(F32)
                    + zr[c, 1, t, h].astype(F32) + zr[c, 2, t, h].astype(F32)
                    for h in range(2)
                )
                yo_own[s, t] = jnp.where(h0 == 0, first, second)
                yo_out[s, t] = jnp.where(h0 == 0, second, first).astype(BF16)
            o_y(c).start()

        @pl.when(c == last)
        def _():
            du_ref[...] = acc_u[...].astype(BF16)
            store_u.start()
            dw_ref[...] = acc_w[...].astype(BF16)
            store_w.start()
            finish(last_sums())
            for t, ref in enumerate((out_ref, ing_ref)):
                total = cr[c, t, z0, h0].astype(F32)
                for place in range(len(PEERS)):
                    total += last_in[place, t].astype(F32)
                ref[last * rows:, :] = total.astype(BF16)

    def total_three(c):
        s = c % SLOTS

        @pl.when(c < last)
        def _():
            finish((o_y(c),))
            at = pl.ds(pl.multiple_of(c * rows, rows), rows)
            out_ref[at, :] = (yo_own[s, 0] + yo_in[c, 0].astype(F32)).astype(BF16)
            ing_ref[at, :] = (yo_own[s, 1] + yo_in[c, 1].astype(F32)).astype(BF16)

    stages = (
        (10, total_three), (9, total_two), (8, total_one), (7, multiply_out), (6, gather_two),
        (5, gather_one), (4, activate), (3, sum_two), (2, sum_one), (1, multiply_in),
        (0, gather_tokens_core), (-1, gather_tokens), (8, add_grads),
    )

    start(first_tokens())
    for c in range(1, CHUNKS):
        tok_y(c).start()
    acc_u[...] = jnp.zeros_like(acc_u)
    acc_w[...] = jnp.zeros_like(acc_w)
    load_u.wait()
    load_w.wait()

    def step(number, carry):
        for behind, stage in stages:
            @pl.when((number >= behind) & (number < behind + CHUNKS))
            def _():
                stage(number - behind)
        return carry

    lax.fori_loop(0, CHUNKS + 9, step, 0)
    store_u.wait()
    store_w.wait()


def hand_on(*refs):
    sources, targets, held, sem = refs[:4], refs[4:8], refs[8:12], refs[12]
    copies = []
    for source, target, room in zip(sources, targets, held):
        parts = max(1, source.shape[0] // 384)
        rows = source.shape[0] // parts
        for number in range(parts):
            at = pl.ds(number * rows, rows)
            place = len(copies)
            copies.append((
                pltpu.make_async_copy(source.at[at], room.at[at], sem.at[0, place]),
                pltpu.make_async_copy(room.at[at], target.at[at], sem.at[1, place]),
            ))
    for load, _ in copies:
        load.start()
    for load, store in copies:
        load.wait()
        store.start()
    for _, store in copies:
        store.wait()


def per_device(inputs, up_weight, down_weight, out_grad):
    tokens, width = inputs.shape
    hidden = up_weight.shape[1]
    rows = tokens // CHUNKS
    owned = rows * 2
    narrow = hidden - WIDE

    def vmem(*shape, dtype=BF16):
        return pltpu.VMEM(shape, dtype)

    scratch = [
        vmem(width, hidden),
        vmem(hidden, width),
        vmem(width, hidden),
        vmem(hidden, width),
        pltpu.SemaphoreType.DMA((6,)),
        vmem(2, CHUNKS, 2, 4, 2, rows, width),
        vmem(HELD, 2, 4, 2, owned, WIDE),
        vmem(HELD, 2, 2, 4, owned, narrow),
        *[vmem(SLOTS, 2, 2, owned, WIDE)] * 3,
        vmem(SLOTS, 2, owned, WIDE),
        vmem(SLOTS, 2, owned, WIDE),
        vmem(SLOTS, 2, owned, WIDE, dtype=F32),
        vmem(SLOTS, 2, 4, owned, narrow),
        *[vmem(SLOTS, 2, owned, narrow)] * 3,
        vmem(2, CHUNKS, 4, 2, owned, WIDE),
        vmem(2, CHUNKS, 2, 4, owned, narrow),
        vmem(HELD, 2, 2, 4, 2, rows, width),
        vmem(CHUNKS, 2, 4, 2, rows, width),
        vmem(CHUNKS, 3, 2, 2, rows, width),
        vmem(len(PEERS), 2, rows, width),
        vmem(SLOTS, 2, rows, width),
        vmem(CHUNKS, 2, rows, width),
        vmem(SLOTS, 2, rows, width, dtype=F32),
        vmem(width, hidden, dtype=F32),
        vmem(hidden, width, dtype=F32),
        pltpu.SemaphoreType.DMA((len(NAMES), SENT)),
        pltpu.SemaphoreType.DMA((len(NAMES), RECEIVED)),
        pltpu.SemaphoreType.DMA((2, 2, len(PEERS))),
        pltpu.SemaphoreType.DMA((2, CHUNKS)),
    ]
    results = (
        jax.ShapeDtypeStruct(inputs.shape, BF16),
        jax.ShapeDtypeStruct(inputs.shape, BF16),
        jax.ShapeDtypeStruct(up_weight.shape, BF16),
        jax.ShapeDtypeStruct(down_weight.shape, BF16),
    )
    near, far = pl.BlockSpec(memory_space=pltpu.VMEM), pl.BlockSpec(memory_space=pl.ANY)
    made = pl.pallas_call(
        kernel,
        out_shape=results,
        in_specs=[far] * 4,
        out_specs=[near, near, far, far],
        scratch_shapes=scratch,
        compiler_params=pltpu.CompilerParams(
            collective_id=0, has_side_effects=True, vmem_limit_bytes=62 * 1024 * 1024
        ),
    )(
        inputs.reshape(CHUNKS, rows, width), up_weight, down_weight,
        out_grad.reshape(CHUNKS, rows, width),
    )
    return pl.pallas_call(
        hand_on,
        out_shape=results,
        in_specs=[far] * 4,
        out_specs=[far] * 4,
        scratch_shapes=[vmem(*one.shape) for one in results] + [pltpu.SemaphoreType.DMA((2, 8))],
        compiler_params=pltpu.CompilerParams(vmem_limit_bytes=62 * 1024 * 1024),
    )(*made)


def solution(mesh):
    placed = (
        P(("ia", "ka"), "ja"),
        P("ja", ("ka", "ia")),
        P(("ka", "ia"), "ja"),
        P(("ia", "ka"), "ja"),
    )
    return jax.shard_map(
        per_device,
        mesh=mesh,
        in_specs=placed,
        out_specs=(
            P(("ia", "ka"), "ja"),
            P(("ia", "ka"), "ja"),
            P("ja", ("ka", "ia")),
            P(("ka", "ia"), "ja"),
        ),
        check_vma=False,
    )
```

```python
import functools

import jax
import jax.numpy as jnp
from jax import lax
from jax.experimental import pallas as pl
from jax.experimental.pallas import tpu as pltpu
from jax.sharding import PartitionSpec as P

sqrt_two_over_pi = 0.7978845608028654
cubic_coeff = 0.044715

MESH = pl.DeviceIdType.MESH
BF16 = jnp.bfloat16
F32 = jnp.float32

CHUNKS = 16
SLOTS = 4
PAIRED = 5
HELD = 3
WIDE = 896

RECEIVED = 3
SENT = 2
EARLY = ("a_t0", "a_t1", "a_d0", "a_d1", "b_y0", "b_y1")
NAMES = (
    "tok_core0", "tok_core1",
    "a_t0", "a_t1", "a_d0", "a_d1", "a_s0", "a_s1", "a_y",
    "b_t0", "b_t1", "b_d0", "b_d1", "b_s0", "b_s1", "b_y0", "b_y1",
    "ga_y", "ga_up", "ga_down", "ga_x0", "ga_x1", "gp_up", "gp_down", "gp_x0", "gp_x1",
    "gb_y0", "gb_y1", "gb_y2", "gb_y3", "gb_up", "gb_down", "gb_x0", "gb_x1",
    "o_core0", "o_core1",
)
def chunk_of(step, turn, half):
    if turn:
        return 3 + step * 2 + half
    return {0: half * 15, 1: 1 + half, 3: 11 + half, 2: 13 + half}[step]


OWN = (chunk_of(0, 0, 0), chunk_of(0, 0, 1))
ACROSS = (chunk_of(0, 1, 0), chunk_of(0, 1, 1))
INDEX = {name: place for place, name in enumerate(EARLY + tuple(n for n in NAMES if n not in EARLY))}


def gelu_pair(preact):
    tanh_inner = jnp.tanh(sqrt_two_over_pi * (preact + cubic_coeff * preact * preact * preact))
    inner_slope = sqrt_two_over_pi * (1.0 + 3.0 * cubic_coeff * preact * preact)
    value = 0.5 * preact * (1.0 + tanh_inner)
    slope = 0.5 * (1.0 + tanh_inner) + 0.5 * preact * (1.0 - tanh_inner * tanh_inner) * inner_slope
    return value, slope


def contract(left, right, dims):
    return lax.dot_general(left, right, (dims, ((), ())), preferred_element_type=F32)


def kernel(
    x_hbm, u_hbm, w_hbm, g_hbm, out_ref, ing_ref, du_hbm, dw_hbm,
    u_ref, w_ref, du_ref, dw_ref, local_sem,
    tok, pa, pb, ta, da, sa, ya_out, ya_in, ya_own, rb, tb, db, sb, ha, hb,
    part, cr, zr, yo_out, yo_in, acc_u, acc_w, send_sem, recv_sem, tok_sem, o_sem, y_sem,
):
    z0 = lax.axis_index("ia")
    ja = lax.axis_index("ja")
    ka = lax.axis_index("ka")
    y0, x0 = ja // 4, ja % 4
    h0, c0 = ka // 2, ka % 2
    rows = x_hbm.shape[1]
    last = CHUNKS - 1
    halves = range(2)

    def at_x(step):
        return (z0, y0 * 4 + (x0 + step + 4) % 4, ka)

    def at_z(step):
        return ((z0 + step + 4) % 4, ja, ka)

    y_pair = (z0, (1 - y0) * 4 + x0, ka)
    h_pair = (z0, ja, (1 - h0) * 2 + c0)
    c_pair = (z0, ja, h0 * 2 + 1 - c0)
    ways = ((0, 1), (1, -1))

    barrier = pltpu.get_barrier_semaphore()
    for other in (at_x(1), at_x(-1), y_pair, c_pair, h_pair, at_z(1), at_z(2), at_z(3)):
        pl.semaphore_signal(barrier, inc=1, device_id=other, device_id_type=MESH)
    loads = [
        pltpu.make_async_copy(ref.at[half], tok.at[t, OWN[half], c0], local_sem.at[t, half])
        for t, ref in enumerate((x_hbm, g_hbm)) for half in halves
    ]
    load_u = pltpu.make_async_copy(u_hbm, u_ref, local_sem.at[2, 0])
    load_w = pltpu.make_async_copy(w_hbm, w_ref, local_sem.at[2, 1])
    spans = (slice(None, WIDE), slice(WIDE, None))
    store_u = [
        pltpu.make_async_copy(du_ref.at[:, span], du_hbm.at[:, span], local_sem.at[3, number])
        for number, span in enumerate(spans)
    ]
    store_w = [
        pltpu.make_async_copy(dw_ref.at[span], dw_hbm.at[span], local_sem.at[4, number])
        for number, span in enumerate(spans)
    ]
    for one in loads + [load_u, load_w]:
        one.start()
    for one in loads:
        one.wait()
    pl.semaphore_wait(barrier, 8)

    def copy(name, c, src, dst, to):
        more = name in EARLY
        sent, received = SENT + more, RECEIVED + more
        place = INDEX[name]
        skipped = 0 if more else len(EARLY)
        return pltpu.make_async_remote_copy(
            src_ref=src, dst_ref=dst,
            send_sem=send_sem.at[place * sent + skipped + c % sent],
            recv_sem=recv_sem.at[place * received + skipped + c % received],
            device_id=to, device_id_type=MESH,
        )

    def gather_first(name, c, ref_of, mine, to):
        return (
            copy(name + "_up", c, ref_of(mine), ref_of(mine), to(1)),
            copy(name + "_down", c, ref_of(mine), ref_of(mine), to(-1)),
        )

    def gather_second(name, c, ref_of, mine, to, axis):
        return tuple(
            copy(name + "_" + axis + str(t), c, ref_of(t, (mine - way + 4) % 4),
                 ref_of(t, (mine - way + 4) % 4), to(way))
            for t, way in ways
        )

    def sum_far(name, c, t, way, piece, transit, mine, to):
        return copy(f"{name}_t{t}", c, piece(t, (mine + 2) % 4), transit.at[t], to(way))

    def sum_near(name, c, t, way, piece, direct, mine, to):
        return copy(f"{name}_d{t}", c, piece(t, (mine - way + 4) % 4), direct.at[t], to(-way))

    def sum_first(name, c, t, way, piece, transit, direct, mine, to):
        return (
            sum_far(name, c, t, way, piece, transit, mine, to),
            sum_near(name, c, t, way, piece, direct, mine, to),
        )

    def sum_second(name, c, t, way, transit, second, to):
        return copy(f"{name}_s{t}", c, transit.at[t], second.at[t], to(way))

    def sum_middle(name, c, piece, transit, direct, second, mine, to):
        for t, way in ways:
            sum_far(name, c, t, way, piece, transit, mine, to).wait_recv()
            transit[t] = (transit[t].astype(F32) + piece(t, (mine + way + 4) % 4)[...].astype(F32)).astype(BF16)
            sum_second(name, c, t, way, transit, second, to).start()

    def sum_last(name, c, piece, transit, direct, second, mine, to):
        totals = []
        for t, way in ways:
            first, straight = sum_first(name, c, t, way, piece, transit, direct, mine, to)
            straight.wait_recv()
            last = sum_second(name, c, t, way, transit, second, to)
            last.wait_recv()
            first.wait_send()
            straight.wait_send()
            last.wait_send()
            totals.append(
                piece(t, mine)[...].astype(F32) + direct[t].astype(F32) + second[t].astype(F32)
            )
        return totals

    def chunk_copy(sem, c, src, dst, to):
        return pltpu.make_async_remote_copy(
            src_ref=src, dst_ref=dst, send_sem=sem.at[0, c], recv_sem=sem.at[1, c],
            device_id=to, device_id_type=MESH,
        )

    def tok_z(step, turn, half):
        c = chunk_of(step, turn, half)
        mine = (ACROSS if turn else OWN)[half]
        return chunk_copy(tok_sem, c, tok.at[:, mine, c0], tok.at[:, c, c0], at_z(-step))

    def tok_y(half):
        c = ACROSS[half]
        return chunk_copy(tok_sem, c, tok.at[:, OWN[half], c0], tok.at[:, c, c0], h_pair)

    def tok_arrived(c):
        here = tok.at[:, c, c0]
        chunk_copy(tok_sem, c, here, here, h_pair).wait_recv()

    def tok_core(c, t):
        here = tok.at[t, c, c0]
        return copy(f"tok_core{t}", c, here, here, c_pair)

    def a_piece(c, t, x):
        return pa.at[c % HELD, t, x]

    def a_args(c):
        s = c % SLOTS
        return functools.partial(a_piece, c), ta.at[s], da.at[s], sa.at[s], x0, at_x

    def a_y(c):
        s = c % SLOTS
        return copy("a_y", c, ya_out.at[s], ya_in.at[s], y_pair)

    def b_y(c, t):
        return copy(f"b_y{t}", c, pb.at[c % HELD, t, 1 - y0], rb.at[c % PAIRED, t], y_pair)

    def b_piece(c, t, x):
        return rb.at[c % PAIRED, t, x]

    def b_args(c):
        s = c % SLOTS
        return functools.partial(b_piece, c), tb.at[s], db.at[s], sb.at[s], x0, at_x

    def ga_y(c):
        here = ha.at[:, c, x0, y0]
        return copy("ga_y", c, here, here, y_pair)

    def gb_y(c, step):
        here = hb.at[:, c, y0, (x0 + step) % 4]
        return copy(f"gb_y{step}", c, here, here, y_pair)

    def ga_first(c):
        return gather_first("ga", c, lambda x: ha.at[:, c, x, y0], x0, at_x)

    def ga_second(c):
        return gather_second("ga", c, lambda t, x: ha.at[t, c, x, y0], x0, at_x, "x")

    def gp_first(c):
        return gather_first("gp", c, lambda x: ha.at[:, c, x, 1 - y0], x0, at_x)

    def gp_second(c):
        return gather_second("gp", c, lambda t, x: ha.at[t, c, x, 1 - y0], x0, at_x, "x")

    def gb_first(c):
        return gather_first("gb", c, lambda x: hb.at[:, c, y0, x], x0, at_x)

    def gb_second(c):
        return gather_second("gb", c, lambda t, x: hb.at[t, c, y0, x], x0, at_x, "x")

    def o_core(c, t):
        return copy(f"o_core{t}", c, part.at[c % HELD, t, 1 - c0], cr.at[c, t], c_pair)

    def o_z(c):
        step = jnp.where(c < 3, 1, jnp.where(c < 11, (c - 3) // 2, 3 - (c - 11) // 2))
        return chunk_copy(o_sem, c, cr.at[c], zr.at[c], ((z0 + step) % 4, ja, ka))

    def o_y():
        return pltpu.make_async_remote_copy(
            src_ref=yo_out, dst_ref=yo_in, send_sem=y_sem.at[0], recv_sem=y_sem.at[1],
            device_id=h_pair, device_id_type=MESH,
        )

    def start(copies):
        for one in copies:
            one.start()

    def finish(copies):
        for one in copies:
            one.wait_recv()
        for one in copies:
            one.wait_send()

    def wide(c, t):
        return tok[t, c].reshape(-1, tok.shape[-1])

    def gather_tokens_core(c):
        @pl.when((c != OWN[1]) & (c != ACROSS[0]) & (c != ACROSS[1]))
        def _():
            tok_arrived(c)

        start([tok_core(c, t) for t in range(2)])

    def multiply_in(c):
        s = c % HELD
        for t, way in ways:
            finish((tok_core(c, t),))
            if t == 0:
                both = contract(wide(c, 0), u_ref[...], ((1,), (0,)))
            else:
                both = contract(wide(c, 1), w_ref[...], ((1,), (1,)))
            both = both.astype(BF16)
            pa[s, t] = both[:, :WIDE].reshape(pa.shape[2:])
            pb[s, t] = both[:, WIDE:].reshape(pb.shape[2:])
            piece, transit, direct, _, mine, to = a_args(c)
            b_y(c, t).start()
            start(sum_first("a", c, t, way, piece, transit, direct, mine, to))

    def sum_one(c):
        sum_middle("a", c, *a_args(c))
        s = c % SLOTS
        piece, transit, direct, _, mine, to = b_args(c)
        for t, way in ways:
            b_y(c, t).wait_recv()
            here = rb.at[c % PAIRED, t]
            here[...] = (here[...].astype(F32) + pb[c % HELD, t, y0].astype(F32)).astype(BF16)
            start(sum_first("b", c, t, way, piece, transit, direct, mine, to))
        for t in range(2):
            b_y(c, t).wait_send()

    def sum_two(c):
        s = c % SLOTS
        totals = sum_last("a", c, *a_args(c))
        for t in range(2):
            first, second = totals[t][0], totals[t][1]
            ya_own[s, t] = jnp.where(y0 == 0, first, second)
            ya_out[s, t] = jnp.where(y0 == 0, second, first).astype(BF16)
        a_y(c).start()
        sum_middle("b", c, *b_args(c))

    def activate(c):
        s = c % SLOTS
        finish((a_y(c),))
        value, slope = gelu_pair(ya_own[s, 0] + ya_in[s, 0].astype(F32))
        ha[0, c, x0, y0] = value.astype(BF16)
        ha[1, c, x0, y0] = ((ya_own[s, 1] + ya_in[s, 1].astype(F32)) * slope).astype(BF16)
        ga_y(c).start()
        start(ga_first(c))
        totals = sum_last("b", c, *b_args(c))
        value, slope = gelu_pair(totals[0])
        hb[0, c, y0, x0] = value.astype(BF16)
        hb[1, c, y0, x0] = (totals[1] * slope).astype(BF16)
        gb_y(c, 0).start()
        start(gb_first(c))

    def gather_one(c):
        finish((ga_y(c),))
        start(gp_first(c))
        finish(gb_first(c))
        start(gb_second(c))
        start((gb_y(c, 1), gb_y(c, 3)))
        finish((gb_y(c, 0),))
        finish(ga_first(c))
        start(ga_second(c))

    def gather_two(c):
        finish(gp_first(c))
        start(gp_second(c))
        finish(gb_second(c))
        gb_y(c, 2).start()
        finish((gb_y(c, 1), gb_y(c, 3)))

    def multiply_out(c):
        finish(ga_second(c))
        finish(gp_second(c))
        finish((gb_y(c, 2),))
        s = c % HELD
        for t in range(2):
            left_a = ha[t, c].reshape(-1, ha.shape[-1])
            left_b = hb[t, c].reshape(-1, hb.shape[-1])
            if t == 0:
                both = contract(left_a, w_ref[:WIDE], ((1,), (0,)))
                both += contract(left_b, w_ref[WIDE:], ((1,), (0,)))
            else:
                both = contract(left_a, u_ref[:, :WIDE], ((1,), (1,)))
                both += contract(left_b, u_ref[:, WIDE:], ((1,), (1,)))
            part[s, t] = both.astype(BF16).reshape(part.shape[2:])
            o_core(c, t).start()

    def add_grads(c):
        def add(flat):
            for span, src in zip(spans, (ha, hb)):
                acc_u[:, span] += contract(flat(tok, 0), flat(src, 1), ((0,), (0,)))
                acc_w[span] += contract(flat(src, 0), flat(tok, 1), ((0,), (0,)))

        @pl.when((c % 2 == 1) & (c < last))
        def _():
            add(lambda ref, t: ref[t, pl.ds(c - 1, 2)].reshape(-1, ref.shape[-1]))

        @pl.when(c == last - 1)
        def _():
            add(lambda ref, t: ref[t, c].reshape(-1, ref.shape[-1]))

    def finish_grads():
        def flat(ref, t):
            return ref[t, last].reshape(-1, ref.shape[-1])

        for number, (span, src) in enumerate(zip(spans, (ha, hb))):
            dw_ref[span] = (acc_w[span] + contract(flat(src, 0), flat(tok, 1), ((0,), (0,)))).astype(BF16)
            store_w[number].start()
            du_ref[:, span] = (acc_u[:, span] + contract(flat(tok, 0), flat(src, 1), ((0,), (0,)))).astype(BF16)
            store_u[number].start()

    def total_one(c):
        s = c % HELD
        for t in range(2):
            finish((o_core(c, t),))
            cr[c, t] = (cr[c, t].astype(F32) + part[s, t, c0].astype(F32)).astype(BF16)

    def total_two(c):
        total_one(c)

        @pl.when((c != OWN[0]) & (c != ACROSS[0]) & (c != ACROSS[1]))
        def _():
            o_z(c).start()

    def sum_parts(first, chunks, t):
        total = first.astype(F32)
        for c in chunks:
            total += zr[c, t].astype(F32)
        return total

    def total_across():
        for half in halves:
            chunks = [chunk_of(step, 1, half) for step in (1, 2, 3)]
            for c in chunks:
                o_z(c).wait_recv()
            for t in range(2):
                yo_out[half, t] = sum_parts(cr[ACROSS[half], t], chunks, t).astype(BF16)
        o_y().start()

    def total_own():
        o_y().wait_recv()
        for half in halves:
            chunks = [chunk_of(step, 0, half) for step in (1, 3, 2)]
            for c in chunks:
                o_z(c).wait_recv()
            at = slice(half * rows, (half + 1) * rows)
            for t, ref in enumerate((out_ref, ing_ref)):
                total = sum_parts(cr[OWN[half], t], chunks, t) + yo_in[half, t].astype(F32)
                ref[at, :] = total.astype(BF16)

    stages = (
        (9, total_two), (8, multiply_out), (7, gather_two), (6, gather_one), (5, activate),
        (4, sum_two), (3, sum_one), (1, multiply_in), (0, gather_tokens_core), (8, add_grads),
    )

    start([tok_core(0, t) for t in range(2)])
    start([tok_z(1, 0, half) for half in halves])
    start([tok_y(half) for half in halves])
    start([tok_z(step, 0, half) for step in (3, 2) for half in halves])
    acc_u[...] = jnp.zeros_like(acc_u)
    acc_w[...] = jnp.zeros_like(acc_w)
    load_u.wait()
    load_w.wait()

    def step(number, carry):
        for behind, stage in stages:
            begin = 1 if stage is gather_tokens_core else behind

            @pl.when((number >= begin) & (number < behind + CHUNKS))
            def _():
                stage(number - behind)

        @pl.when(number == 2)
        def _():
            for half in halves:
                tok_arrived(ACROSS[half])
                start([tok_z(other, 1, half) for other in (1, 2, 3)])

        @pl.when(number == chunk_of(3, 1, 1) + 11)
        def _():
            total_across()

        return carry

    lax.fori_loop(0, CHUNKS + 8, step, 0)
    finish_grads()
    total_one(last)
    total_own()
    for half in halves:
        tok_y(half).wait_send()
        for other in (1, 2, 3):
            tok_z(other, 0, half).wait_send()
            tok_z(other, 1, half).wait_send()
            o_z(chunk_of(other, 0, half)).wait_send()
            o_z(chunk_of(other, 1, half)).wait_send()
    o_y().wait_send()
    for one in store_u + store_w:
        one.wait()


def hand_on(*refs):
    sources, targets, held, sem = refs[:4], refs[4:8], refs[8:12], refs[12]
    copies = []
    for source, target, room in zip(sources, targets, held):
        parts = max(1, source.shape[0] // 384)
        rows = source.shape[0] // parts
        for number in range(parts):
            at = pl.ds(number * rows, rows)
            place = len(copies)
            copies.append((
                pltpu.make_async_copy(source.at[at], room.at[at], sem.at[0, place]),
                pltpu.make_async_copy(room.at[at], target.at[at], sem.at[1, place]),
            ))
    for load, _ in copies:
        load.start()
    for load, store in copies:
        load.wait()
        store.start()
    for _, store in copies:
        store.wait()


def per_device(inputs, up_weight, down_weight, out_grad):
    tokens, width = inputs.shape
    hidden = up_weight.shape[1]
    rows = tokens // 2
    owned = rows // 4
    narrow = hidden - WIDE

    def vmem(*shape, dtype=BF16):
        return pltpu.VMEM(shape, dtype)

    scratch = [
        vmem(width, hidden),
        vmem(hidden, width),
        vmem(width, hidden),
        vmem(hidden, width),
        pltpu.SemaphoreType.DMA((5, 2)),
        vmem(2, CHUNKS, 2, rows, width),
        vmem(HELD, 2, 4, 2, owned, WIDE),
        vmem(HELD, 2, 2, 4, owned, narrow),
        *[vmem(SLOTS, 2, 2, owned, WIDE)] * 3,
        vmem(SLOTS, 2, owned, WIDE),
        vmem(SLOTS, 2, owned, WIDE),
        vmem(SLOTS, 2, owned, WIDE, dtype=F32),
        vmem(PAIRED, 2, 4, owned, narrow),
        *[vmem(SLOTS, 2, owned, narrow)] * 3,
        vmem(2, CHUNKS, 4, 2, owned, WIDE),
        vmem(2, CHUNKS, 2, 4, owned, narrow),
        vmem(HELD, 2, 2, rows, width),
        vmem(CHUNKS, 2, rows, width),
        vmem(CHUNKS, 2, rows, width),
        vmem(2, 2, rows, width),
        vmem(2, 2, rows, width),
        vmem(width, hidden, dtype=F32),
        vmem(hidden, width, dtype=F32),
        pltpu.SemaphoreType.DMA((len(NAMES) * SENT + len(EARLY),)),
        pltpu.SemaphoreType.DMA((len(NAMES) * RECEIVED + len(EARLY),)),
        *[pltpu.SemaphoreType.DMA((2, CHUNKS))] * 2,
        pltpu.SemaphoreType.DMA((2,)),
    ]
    results = (
        jax.ShapeDtypeStruct(inputs.shape, BF16),
        jax.ShapeDtypeStruct(inputs.shape, BF16),
        jax.ShapeDtypeStruct(up_weight.shape, BF16),
        jax.ShapeDtypeStruct(down_weight.shape, BF16),
    )
    near, far = pl.BlockSpec(memory_space=pltpu.VMEM), pl.BlockSpec(memory_space=pl.ANY)
    made = pl.pallas_call(
        kernel,
        out_shape=results,
        in_specs=[far] * 4,
        out_specs=[near, near, far, far],
        scratch_shapes=scratch,
        compiler_params=pltpu.CompilerParams(
            collective_id=0, has_side_effects=True, vmem_limit_bytes=62 * 1024 * 1024
        ),
    )(
        inputs.reshape(2, rows, width), up_weight, down_weight,
        out_grad.reshape(2, rows, width),
    )
    return pl.pallas_call(
        hand_on,
        out_shape=results,
        in_specs=[far] * 4,
        out_specs=[far] * 4,
        scratch_shapes=[vmem(*one.shape) for one in results] + [pltpu.SemaphoreType.DMA((2, 8))],
        compiler_params=pltpu.CompilerParams(vmem_limit_bytes=62 * 1024 * 1024),
    )(*made)


def solution(mesh):
    placed = (
        P(("ia", "ka"), "ja"),
        P("ja", ("ka", "ia")),
        P(("ka", "ia"), "ja"),
        P(("ia", "ka"), "ja"),
    )
    return jax.shard_map(
        per_device,
        mesh=mesh,
        in_specs=placed,
        out_specs=(
            P(("ia", "ka"), "ja"),
            P(("ia", "ka"), "ja"),
            P("ja", ("ka", "ia")),
            P(("ka", "ia"), "ja"),
        ),
        check_vma=False,
    )
```

```python
import functools

import jax
import jax.numpy as jnp
from jax import lax
from jax.experimental import pallas as pl
from jax.experimental.pallas import tpu as pltpu
from jax.sharding import PartitionSpec as P

sqrt_two_over_pi = 0.7978845608028654
cubic_coeff = 0.044715

MESH = pl.DeviceIdType.MESH
BF16 = jnp.bfloat16
F32 = jnp.float32

CHUNKS = 16
SLOTS = 4
PAIRED = 5
HELD = 3
WIDE = 896

RECEIVED = 3
SENT = 2
EARLY = ("a_t0", "a_t1", "a_d0", "a_d1", "b_y0", "b_y1")
NAMES = (
    "tok_core0", "tok_core1",
    "a_t0", "a_t1", "a_d0", "a_d1", "a_s0", "a_s1", "a_y",
    "b_t0", "b_t1", "b_d0", "b_d1", "b_s0", "b_s1", "b_y0", "b_y1",
    "ga_y", "ga_up", "ga_down", "ga_x0", "ga_x1", "gp_up", "gp_down", "gp_x0", "gp_x1",
    "gb_y0", "gb_y1", "gb_y2", "gb_y3", "gb_up", "gb_down", "gb_x0", "gb_x1",
    "o_core0", "o_core1",
)
def chunk_of(step, turn, half):
    if turn:
        return 3 + step * 2 + half
    return {0: half * 15, 1: 1 + half, 2: 11 + half, 3: 13 + half}[step]


OWN = (chunk_of(0, 0, 0), chunk_of(0, 0, 1))
ACROSS = (chunk_of(0, 1, 0), chunk_of(0, 1, 1))
INDEX = {name: place for place, name in enumerate(EARLY + tuple(n for n in NAMES if n not in EARLY))}


def gelu_pair(preact):
    tanh_inner = jnp.tanh(sqrt_two_over_pi * (preact + cubic_coeff * preact * preact * preact))
    inner_slope = sqrt_two_over_pi * (1.0 + 3.0 * cubic_coeff * preact * preact)
    value = 0.5 * preact * (1.0 + tanh_inner)
    slope = 0.5 * (1.0 + tanh_inner) + 0.5 * preact * (1.0 - tanh_inner * tanh_inner) * inner_slope
    return value, slope


def contract(left, right, dims):
    return lax.dot_general(left, right, (dims, ((), ())), preferred_element_type=F32)


def kernel(
    x_hbm, u_hbm, w_hbm, g_hbm, out_ref, ing_ref, du_hbm, dw_hbm,
    u_ref, w_ref, du_ref, dw_ref, local_sem,
    tok, pa, pb, ta, da, sa, ya_out, ya_in, ya_own, rb, tb, db, sb, ha, hb,
    part, cr, zr, yo_out, yo_in, acc_u, acc_w, send_sem, recv_sem, tok_sem, o_sem, y_sem, far_sem,
):
    z0 = lax.axis_index("ia")
    ja = lax.axis_index("ja")
    ka = lax.axis_index("ka")
    y0, x0 = ja // 4, ja % 4
    h0, c0 = ka // 2, ka % 2
    rows = x_hbm.shape[1]
    last = CHUNKS - 1
    halves = range(2)

    def at_x(step):
        return (z0, y0 * 4 + (x0 + step + 4) % 4, ka)

    def at_z(step):
        return ((z0 + step + 4) % 4, ja, ka)

    y_pair = (z0, (1 - y0) * 4 + x0, ka)
    h_pair = (z0, ja, (1 - h0) * 2 + c0)
    c_pair = (z0, ja, h0 * 2 + 1 - c0)
    ways = ((0, 1), (1, -1))

    barrier = pltpu.get_barrier_semaphore()
    for other in (at_x(1), at_x(-1), y_pair, c_pair, h_pair, at_z(1), at_z(2), at_z(3)):
        pl.semaphore_signal(barrier, inc=1, device_id=other, device_id_type=MESH)
    loads = [
        pltpu.make_async_copy(ref.at[half], tok.at[t, OWN[half], c0], local_sem.at[t, half])
        for t, ref in enumerate((x_hbm, g_hbm)) for half in halves
    ]
    load_u = pltpu.make_async_copy(u_hbm, u_ref, local_sem.at[2, 0])
    load_w = pltpu.make_async_copy(w_hbm, w_ref, local_sem.at[2, 1])
    spans = (slice(None, WIDE), slice(WIDE, None))
    store_u = [
        pltpu.make_async_copy(du_ref.at[:, span], du_hbm.at[:, span], local_sem.at[3, number])
        for number, span in enumerate(spans)
    ]
    store_w = [
        pltpu.make_async_copy(dw_ref.at[span], dw_hbm.at[span], local_sem.at[4, number])
        for number, span in enumerate(spans)
    ]
    for one in loads + [load_u, load_w]:
        one.start()
    for one in loads:
        one.wait()
    pl.semaphore_wait(barrier, 8)

    def copy(name, c, src, dst, to):
        more = name in EARLY
        sent, received = SENT + more, RECEIVED + more
        place = INDEX[name]
        skipped = 0 if more else len(EARLY)
        return pltpu.make_async_remote_copy(
            src_ref=src, dst_ref=dst,
            send_sem=send_sem.at[place * sent + skipped + c % sent],
            recv_sem=recv_sem.at[place * received + skipped + c % received],
            device_id=to, device_id_type=MESH,
        )

    def gather_first(name, c, ref_of, mine, to):
        return (
            copy(name + "_up", c, ref_of(mine), ref_of(mine), to(1)),
            copy(name + "_down", c, ref_of(mine), ref_of(mine), to(-1)),
        )

    def gather_second(name, c, ref_of, mine, to, axis):
        return tuple(
            copy(name + "_" + axis + str(t), c, ref_of(t, (mine - way + 4) % 4),
                 ref_of(t, (mine - way + 4) % 4), to(way))
            for t, way in ways
        )

    def sum_far(name, c, t, way, piece, transit, mine, to):
        return copy(f"{name}_t{t}", c, piece(t, (mine + 2) % 4), transit.at[t], to(way))

    def sum_near(name, c, t, way, piece, direct, mine, to):
        return copy(f"{name}_d{t}", c, piece(t, (mine - way + 4) % 4), direct.at[t], to(-way))

    def sum_first(name, c, t, way, piece, transit, direct, mine, to):
        return (
            sum_far(name, c, t, way, piece, transit, mine, to),
            sum_near(name, c, t, way, piece, direct, mine, to),
        )

    def sum_second(name, c, t, way, transit, second, to):
        return copy(f"{name}_s{t}", c, transit.at[t], second.at[t], to(way))

    def sum_middle(name, c, piece, transit, direct, second, mine, to):
        for t, way in ways:
            sum_far(name, c, t, way, piece, transit, mine, to).wait_recv()
            transit[t] = (transit[t].astype(F32) + piece(t, (mine + way + 4) % 4)[...].astype(F32)).astype(BF16)
            sum_second(name, c, t, way, transit, second, to).start()

    def sum_last(name, c, piece, transit, direct, second, mine, to):
        totals = []
        for t, way in ways:
            first, straight = sum_first(name, c, t, way, piece, transit, direct, mine, to)
            straight.wait_recv()
            last = sum_second(name, c, t, way, transit, second, to)
            last.wait_recv()
            first.wait_send()
            straight.wait_send()
            last.wait_send()
            totals.append(
                piece(t, mine)[...].astype(F32) + direct[t].astype(F32) + second[t].astype(F32)
            )
        return totals

    def chunk_copy(sem, c, src, dst, to):
        return pltpu.make_async_remote_copy(
            src_ref=src, dst_ref=dst, send_sem=sem.at[0, c], recv_sem=sem.at[1, c],
            device_id=to, device_id_type=MESH,
        )

    def tok_z(step, turn, half):
        c = chunk_of(step, turn, half)
        mine = (ACROSS if turn else OWN)[half]
        return chunk_copy(tok_sem, c, tok.at[:, mine, c0], tok.at[:, c, c0], at_z(-step))

    def tok_y(half):
        c = ACROSS[half]
        return chunk_copy(tok_sem, c, tok.at[:, OWN[half], c0], tok.at[:, c, c0], h_pair)

    def tok_arrived(c):
        here = tok.at[:, c, c0]
        chunk_copy(tok_sem, c, here, here, h_pair).wait_recv()

    def tok_core(c, t):
        here = tok.at[t, c, c0]
        return copy(f"tok_core{t}", c, here, here, c_pair)

    def a_piece(c, t, x):
        return pa.at[c % HELD, t, x]

    def a_args(c):
        s = c % SLOTS
        return functools.partial(a_piece, c), ta.at[s], da.at[s], sa.at[s], x0, at_x

    def a_y(c):
        s = c % SLOTS
        return copy("a_y", c, ya_out.at[s], ya_in.at[s], y_pair)

    def b_y(c, t):
        return copy(f"b_y{t}", c, pb.at[c % HELD, t, 1 - y0], rb.at[c % PAIRED, t], y_pair)

    def b_piece(c, t, x):
        return rb.at[c % PAIRED, t, x]

    def b_args(c):
        s = c % SLOTS
        return functools.partial(b_piece, c), tb.at[s], db.at[s], sb.at[s], x0, at_x

    def ga_y(c):
        here = ha.at[:, c, x0, y0]
        return copy("ga_y", c, here, here, y_pair)

    def gb_y(c, step):
        here = hb.at[:, c, y0, (x0 + step) % 4]
        return copy(f"gb_y{step}", c, here, here, y_pair)

    def ga_first(c):
        return gather_first("ga", c, lambda x: ha.at[:, c, x, y0], x0, at_x)

    def ga_second(c):
        return gather_second("ga", c, lambda t, x: ha.at[t, c, x, y0], x0, at_x, "x")

    def gp_first(c):
        return gather_first("gp", c, lambda x: ha.at[:, c, x, 1 - y0], x0, at_x)

    def gp_second(c):
        return gather_second("gp", c, lambda t, x: ha.at[t, c, x, 1 - y0], x0, at_x, "x")

    def gb_first(c):
        return gather_first("gb", c, lambda x: hb.at[:, c, y0, x], x0, at_x)

    def gb_second(c):
        return gather_second("gb", c, lambda t, x: hb.at[t, c, y0, x], x0, at_x, "x")

    def far_copy(number, src):
        return pltpu.make_async_remote_copy(
            src_ref=src, dst_ref=src, send_sem=far_sem.at[0, number], recv_sem=far_sem.at[1, number],
            device_id=at_x(2), device_id_type=MESH,
        )

    def ga_far():
        return far_copy(0, ha.at[:, last, x0, y0])

    def gp_far():
        return far_copy(1, ha.at[:, last, x0, 1 - y0])

    def gb_far():
        return far_copy(2, hb.at[:, last, y0, x0])

    def o_core(c, t):
        return copy(f"o_core{t}", c, part.at[c % HELD, t, 1 - c0], cr.at[c, t], c_pair)

    def o_z(c):
        step = jnp.where(c < 3, 1, jnp.where(c < 11, (c - 3) // 2, 2 + (c - 11) // 2))
        return chunk_copy(o_sem, c, cr.at[c], zr.at[c], ((z0 + step) % 4, ja, ka))

    def o_y():
        return pltpu.make_async_remote_copy(
            src_ref=yo_out, dst_ref=yo_in, send_sem=y_sem.at[0], recv_sem=y_sem.at[1],
            device_id=h_pair, device_id_type=MESH,
        )

    def start(copies):
        for one in copies:
            one.start()

    def finish(copies):
        for one in copies:
            one.wait_recv()
        for one in copies:
            one.wait_send()

    def wide(c, t):
        return tok[t, c].reshape(-1, tok.shape[-1])

    def gather_tokens_core(c):
        @pl.when((c != OWN[1]) & (c != ACROSS[0]) & (c != ACROSS[1]))
        def _():
            tok_arrived(c)

        start([tok_core(c, t) for t in range(2)])

    def multiply_in(c):
        s = c % HELD
        for t, way in ways:
            finish((tok_core(c, t),))
            if t == 0:
                both = contract(wide(c, 0), u_ref[...], ((1,), (0,)))
            else:
                both = contract(wide(c, 1), w_ref[...], ((1,), (1,)))
            both = both.astype(BF16)
            pa[s, t] = both[:, :WIDE].reshape(pa.shape[2:])
            pb[s, t] = both[:, WIDE:].reshape(pb.shape[2:])
            piece, transit, direct, _, mine, to = a_args(c)
            b_y(c, t).start()
            start(sum_first("a", c, t, way, piece, transit, direct, mine, to))

    def sum_one(c):
        sum_middle("a", c, *a_args(c))
        s = c % SLOTS
        piece, transit, direct, _, mine, to = b_args(c)
        for t, way in ways:
            b_y(c, t).wait_recv()
            here = rb.at[c % PAIRED, t]
            here[...] = (here[...].astype(F32) + pb[c % HELD, t, y0].astype(F32)).astype(BF16)
            start(sum_first("b", c, t, way, piece, transit, direct, mine, to))
        for t in range(2):
            b_y(c, t).wait_send()

    def sum_two(c):
        s = c % SLOTS
        totals = sum_last("a", c, *a_args(c))
        for t in range(2):
            first, second = totals[t][0], totals[t][1]
            ya_own[s, t] = jnp.where(y0 == 0, first, second)
            ya_out[s, t] = jnp.where(y0 == 0, second, first).astype(BF16)
        a_y(c).start()
        sum_middle("b", c, *b_args(c))

    def activate(c):
        s = c % SLOTS
        finish((a_y(c),))
        value, slope = gelu_pair(ya_own[s, 0] + ya_in[s, 0].astype(F32))
        ha[0, c, x0, y0] = value.astype(BF16)
        ha[1, c, x0, y0] = ((ya_own[s, 1] + ya_in[s, 1].astype(F32)) * slope).astype(BF16)
        ga_y(c).start()
        start(ga_first(c))
        totals = sum_last("b", c, *b_args(c))
        value, slope = gelu_pair(totals[0])
        hb[0, c, y0, x0] = value.astype(BF16)
        hb[1, c, y0, x0] = (totals[1] * slope).astype(BF16)
        gb_y(c, 0).start()
        start(gb_first(c))

        @pl.when(c == last)
        def _():
            start((ga_far(), gb_far()))

    def gather_one(c):
        finish((ga_y(c),))
        start(gp_first(c))

        @pl.when(c == last)
        def _():
            gp_far().start()

        finish(gb_first(c))

        @pl.when(c < last)
        def _():
            start(gb_second(c))

        start((gb_y(c, 1), gb_y(c, 3)))

        @pl.when(c == last)
        def _():
            finish((gb_far(),))
            gb_y(c, 2).start()

        finish((gb_y(c, 0),))
        finish(ga_first(c))

        @pl.when(c < last)
        def _():
            start(ga_second(c))

        @pl.when(c == last)
        def _():
            finish((ga_far(),))

    def gather_two(c):
        finish(gp_first(c))
        start(gp_second(c))
        finish(gb_second(c))
        gb_y(c, 2).start()
        finish((gb_y(c, 1), gb_y(c, 3)))

    def multiply_out(c):
        finish(ga_second(c))
        finish(gp_second(c))
        finish((gb_y(c, 2),))
        multiply_gathered(c)

    def multiply_last():
        finish(gp_first(last))
        finish((gp_far(),))
        finish([gb_y(last, step) for step in (1, 2, 3)])
        multiply_gathered(last)

    def multiply_gathered(c):
        s = c % HELD
        for t in range(2):
            left_a = ha[t, c].reshape(-1, ha.shape[-1])
            left_b = hb[t, c].reshape(-1, hb.shape[-1])
            if t == 0:
                both = contract(left_a, w_ref[:WIDE], ((1,), (0,)))
                both += contract(left_b, w_ref[WIDE:], ((1,), (0,)))
            else:
                both = contract(left_a, u_ref[:, :WIDE], ((1,), (1,)))
                both += contract(left_b, u_ref[:, WIDE:], ((1,), (1,)))
            part[s, t] = both.astype(BF16).reshape(part.shape[2:])
            o_core(c, t).start()

    def add_grads(c):
        def add(flat):
            for span, src in zip(spans, (ha, hb)):
                acc_u[:, span] += contract(flat(tok, 0), flat(src, 1), ((0,), (0,)))
                acc_w[span] += contract(flat(src, 0), flat(tok, 1), ((0,), (0,)))

        @pl.when((c % 2 == 1) & (c < last))
        def _():
            add(lambda ref, t: ref[t, pl.ds(c - 1, 2)].reshape(-1, ref.shape[-1]))

        @pl.when(c == last - 1)
        def _():
            add(lambda ref, t: ref[t, c].reshape(-1, ref.shape[-1]))

    def finish_grads():
        def flat(ref, t):
            return ref[t, last].reshape(-1, ref.shape[-1])

        for number, (span, src) in enumerate(zip(spans, (ha, hb))):
            dw_ref[span] = (acc_w[span] + contract(flat(src, 0), flat(tok, 1), ((0,), (0,)))).astype(BF16)
            store_w[number].start()
            du_ref[:, span] = (acc_u[:, span] + contract(flat(tok, 0), flat(src, 1), ((0,), (0,)))).astype(BF16)
            store_u[number].start()

    def total_one(c):
        s = c % HELD
        for t in range(2):
            finish((o_core(c, t),))
            cr[c, t] = (cr[c, t].astype(F32) + part[s, t, c0].astype(F32)).astype(BF16)

    def total_two(c):
        total_one(c)

        @pl.when((c != OWN[0]) & (c != ACROSS[0]) & (c != ACROSS[1]))
        def _():
            o_z(c).start()

    def sum_parts(first, chunks, t):
        total = first.astype(F32)
        for c in chunks:
            total += zr[c, t].astype(F32)
        return total

    def total_across():
        for half in halves:
            chunks = [chunk_of(step, 1, half) for step in (1, 2, 3)]
            for c in chunks:
                o_z(c).wait_recv()
            for t in range(2):
                yo_out[half, t] = sum_parts(cr[ACROSS[half], t], chunks, t).astype(BF16)
        o_y().start()

    def total_own():
        o_y().wait_recv()
        for half in halves:
            chunks = [chunk_of(step, 0, half) for step in (1, 2, 3)]
            for c in chunks:
                o_z(c).wait_recv()
            at = slice(half * rows, (half + 1) * rows)
            for t, ref in enumerate((out_ref, ing_ref)):
                total = sum_parts(cr[OWN[half], t], chunks, t) + yo_in[half, t].astype(F32)
                ref[at, :] = total.astype(BF16)

    stages = (
        (9, total_two), (8, multiply_out), (7, gather_two), (6, gather_one), (5, activate),
        (4, sum_two), (3, sum_one), (1, multiply_in), (0, gather_tokens_core), (8, add_grads),
    )

    start([tok_core(0, t) for t in range(2)])
    start([tok_z(1, 0, half) for half in halves])
    start([tok_y(half) for half in halves])
    start([tok_z(step, 0, half) for step in (2, 3) for half in halves])
    acc_u[...] = jnp.zeros_like(acc_u)
    acc_w[...] = jnp.zeros_like(acc_w)
    load_u.wait()
    load_w.wait()

    def step(number, carry):
        for behind, stage in stages:
            begin = 1 if stage is gather_tokens_core else behind

            count = CHUNKS - 1 if stage is gather_two else CHUNKS

            @pl.when((number >= begin) & (number < behind + count))
            def _():
                stage(number - behind)

        @pl.when(number == 2)
        def _():
            for half in halves:
                tok_arrived(ACROSS[half])
                start([tok_z(other, 1, half) for other in (1, 2, 3)])

        @pl.when(number == chunk_of(3, 1, 1) + 11)
        def _():
            total_across()

        return carry

    lax.fori_loop(0, CHUNKS + 7, step, 0)
    total_two(last - 1)
    multiply_last()
    finish_grads()
    total_one(last)
    total_own()
    for half in halves:
        tok_y(half).wait_send()
        for other in (1, 2, 3):
            tok_z(other, 0, half).wait_send()
            tok_z(other, 1, half).wait_send()
            o_z(chunk_of(other, 0, half)).wait_send()
            o_z(chunk_of(other, 1, half)).wait_send()
    o_y().wait_send()
    for one in store_u + store_w:
        one.wait()


def hand_on(*refs):
    sources, targets, held, sem = refs[:4], refs[4:8], refs[8:12], refs[12]
    copies = []
    for source, target, room in zip(sources, targets, held):
        parts = max(1, source.shape[0] // 384)
        rows = source.shape[0] // parts
        for number in range(parts):
            at = pl.ds(number * rows, rows)
            place = len(copies)
            copies.append((
                pltpu.make_async_copy(source.at[at], room.at[at], sem.at[0, place]),
                pltpu.make_async_copy(room.at[at], target.at[at], sem.at[1, place]),
            ))
    for load, _ in copies:
        load.start()
    for load, store in copies:
        load.wait()
        store.start()
    for _, store in copies:
        store.wait()


def per_device(inputs, up_weight, down_weight, out_grad):
    tokens, width = inputs.shape
    hidden = up_weight.shape[1]
    rows = tokens // 2
    owned = rows // 4
    narrow = hidden - WIDE

    def vmem(*shape, dtype=BF16):
        return pltpu.VMEM(shape, dtype)

    scratch = [
        vmem(width, hidden),
        vmem(hidden, width),
        vmem(width, hidden),
        vmem(hidden, width),
        pltpu.SemaphoreType.DMA((5, 2)),
        vmem(2, CHUNKS, 2, rows, width),
        vmem(HELD, 2, 4, 2, owned, WIDE),
        vmem(HELD, 2, 2, 4, owned, narrow),
        *[vmem(SLOTS, 2, 2, owned, WIDE)] * 3,
        vmem(SLOTS, 2, owned, WIDE),
        vmem(SLOTS, 2, owned, WIDE),
        vmem(SLOTS, 2, owned, WIDE, dtype=F32),
        vmem(PAIRED, 2, 4, owned, narrow),
        *[vmem(SLOTS, 2, owned, narrow)] * 3,
        vmem(2, CHUNKS, 4, 2, owned, WIDE),
        vmem(2, CHUNKS, 2, 4, owned, narrow),
        vmem(HELD, 2, 2, rows, width),
        vmem(CHUNKS, 2, rows, width),
        vmem(CHUNKS, 2, rows, width),
        vmem(2, 2, rows, width),
        vmem(2, 2, rows, width),
        vmem(width, hidden, dtype=F32),
        vmem(hidden, width, dtype=F32),
        pltpu.SemaphoreType.DMA((len(NAMES) * SENT + len(EARLY),)),
        pltpu.SemaphoreType.DMA((len(NAMES) * RECEIVED + len(EARLY),)),
        *[pltpu.SemaphoreType.DMA((2, CHUNKS))] * 2,
        pltpu.SemaphoreType.DMA((2,)),
        pltpu.SemaphoreType.DMA((2, 3)),
    ]
    results = (
        jax.ShapeDtypeStruct(inputs.shape, BF16),
        jax.ShapeDtypeStruct(inputs.shape, BF16),
        jax.ShapeDtypeStruct(up_weight.shape, BF16),
        jax.ShapeDtypeStruct(down_weight.shape, BF16),
    )
    near, far = pl.BlockSpec(memory_space=pltpu.VMEM), pl.BlockSpec(memory_space=pl.ANY)
    made = pl.pallas_call(
        kernel,
        out_shape=results,
        in_specs=[far] * 4,
        out_specs=[near, near, far, far],
        scratch_shapes=scratch,
        compiler_params=pltpu.CompilerParams(
            collective_id=0, has_side_effects=True, vmem_limit_bytes=62 * 1024 * 1024
        ),
    )(
        inputs.reshape(2, rows, width), up_weight, down_weight,
        out_grad.reshape(2, rows, width),
    )
    return pl.pallas_call(
        hand_on,
        out_shape=results,
        in_specs=[far] * 4,
        out_specs=[far] * 4,
        scratch_shapes=[vmem(*one.shape) for one in results] + [pltpu.SemaphoreType.DMA((2, 8))],
        compiler_params=pltpu.CompilerParams(vmem_limit_bytes=62 * 1024 * 1024),
    )(*made)


def solution(mesh):
    placed = (
        P(("ia", "ka"), "ja"),
        P("ja", ("ka", "ia")),
        P(("ka", "ia"), "ja"),
        P(("ia", "ka"), "ja"),
    )
    return jax.shard_map(
        per_device,
        mesh=mesh,
        in_specs=placed,
        out_specs=(
            P(("ia", "ka"), "ja"),
            P(("ia", "ka"), "ja"),
            P("ja", ("ka", "ia")),
            P(("ka", "ia"), "ja"),
        ),
        check_vma=False,
    )
```

```python
import functools

import jax
import jax.numpy as jnp
from jax import lax
from jax.experimental import pallas as pl
from jax.experimental.pallas import tpu as pltpu
from jax.sharding import PartitionSpec as P

sqrt_two_over_pi = 0.7978845608028654
cubic_coeff = 0.044715

MESH = pl.DeviceIdType.MESH
BF16 = jnp.bfloat16
F32 = jnp.float32

CHUNKS = 16
SLOTS = 4
PAIRED = 5
HELD = 3
WIDE = 896

RECEIVED = 3
SENT = 2
EARLY = ("a_t0", "a_t1", "a_d0", "a_d1", "b_y0", "b_y1")
NAMES = (
    "tok_core0", "tok_core1",
    "a_t0", "a_t1", "a_d0", "a_d1", "a_s0", "a_s1", "a_y",
    "b_t0", "b_t1", "b_d0", "b_d1", "b_s0", "b_s1", "b_y0", "b_y1",
    "ga_y", "ga_up", "ga_down", "ga_x0", "ga_x1", "gp_up", "gp_down", "gp_x0", "gp_x1",
    "gb_y0", "gb_y1", "gb_y2", "gb_y3", "gb_up", "gb_down", "gb_x0", "gb_x1",
    "o_core0", "o_core1",
)
def chunk_of(step, turn, half):
    if turn:
        return 3 + step * 2 + half
    return {0: half * 15, 1: 1 + half, 2: 11 + half, 3: 13 + half}[step]


OWN = (chunk_of(0, 0, 0), chunk_of(0, 0, 1))
ACROSS = (chunk_of(0, 1, 0), chunk_of(0, 1, 1))
INDEX = {name: place for place, name in enumerate(EARLY + tuple(n for n in NAMES if n not in EARLY))}


def gelu_pair(preact):
    tanh_inner = jnp.tanh(sqrt_two_over_pi * (preact + cubic_coeff * preact * preact * preact))
    inner_slope = sqrt_two_over_pi * (1.0 + 3.0 * cubic_coeff * preact * preact)
    value = 0.5 * preact * (1.0 + tanh_inner)
    slope = 0.5 * (1.0 + tanh_inner) + 0.5 * preact * (1.0 - tanh_inner * tanh_inner) * inner_slope
    return value, slope


def contract(left, right, dims):
    return lax.dot_general(left, right, (dims, ((), ())), preferred_element_type=F32)


def kernel(
    x_hbm, u_hbm, w_hbm, g_hbm, out_ref, ing_ref, du_hbm, dw_hbm,
    u_ref, w_ref, du_ref, dw_ref, local_sem,
    tok, pa, pb, ta, da, sa, ya_out, ya_in, ya_own, rb, tb, db, sb, ha, hb,
    part, cr, zr, yo_out, yo_in, acc_u, acc_w, send_sem, recv_sem, tok_sem, o_sem, y_sem, far_sem,
):
    z0 = lax.axis_index("ia")
    ja = lax.axis_index("ja")
    ka = lax.axis_index("ka")
    y0, x0 = ja // 4, ja % 4
    h0, c0 = ka // 2, ka % 2
    rows = x_hbm.shape[1]
    last = CHUNKS - 1
    halves = range(2)

    def at_x(step):
        return (z0, y0 * 4 + (x0 + step + 4) % 4, ka)

    def at_z(step):
        return ((z0 + step + 4) % 4, ja, ka)

    y_pair = (z0, (1 - y0) * 4 + x0, ka)
    h_pair = (z0, ja, (1 - h0) * 2 + c0)
    c_pair = (z0, ja, h0 * 2 + 1 - c0)
    ways = ((0, 1), (1, -1))

    barrier = pltpu.get_barrier_semaphore()
    for other in (at_x(1), at_x(-1), y_pair, c_pair, h_pair, at_z(1), at_z(2), at_z(3)):
        pl.semaphore_signal(barrier, inc=1, device_id=other, device_id_type=MESH)
    loads = [
        pltpu.make_async_copy(ref.at[half], tok.at[t, OWN[half], c0], local_sem.at[t, half])
        for t, ref in enumerate((x_hbm, g_hbm)) for half in halves
    ]
    load_u = pltpu.make_async_copy(u_hbm, u_ref, local_sem.at[2, 0])
    load_w = pltpu.make_async_copy(w_hbm, w_ref, local_sem.at[2, 1])
    spans = (slice(None, WIDE), slice(WIDE, None))
    store_u = [
        pltpu.make_async_copy(du_ref.at[:, span], du_hbm.at[:, span], local_sem.at[3, number])
        for number, span in enumerate(spans)
    ]
    store_w = [
        pltpu.make_async_copy(dw_ref.at[span], dw_hbm.at[span], local_sem.at[4, number])
        for number, span in enumerate(spans)
    ]
    for one in loads + [load_u, load_w]:
        one.start()
    for one in loads:
        one.wait()
    pl.semaphore_wait(barrier, 8)

    def copy(name, c, src, dst, to):
        more = name in EARLY
        sent, received = SENT + more, RECEIVED + more
        place = INDEX[name]
        skipped = 0 if more else len(EARLY)
        return pltpu.make_async_remote_copy(
            src_ref=src, dst_ref=dst,
            send_sem=send_sem.at[place * sent + skipped + c % sent],
            recv_sem=recv_sem.at[place * received + skipped + c % received],
            device_id=to, device_id_type=MESH,
        )

    def gather_first(name, c, ref_of, mine, to):
        return (
            copy(name + "_up", c, ref_of(mine), ref_of(mine), to(1)),
            copy(name + "_down", c, ref_of(mine), ref_of(mine), to(-1)),
        )

    def gather_second(name, c, ref_of, mine, to, axis):
        return tuple(
            copy(name + "_" + axis + str(t), c, ref_of(t, (mine - way + 4) % 4),
                 ref_of(t, (mine - way + 4) % 4), to(way))
            for t, way in ways
        )

    def sum_far(name, c, t, way, piece, transit, mine, to):
        return copy(f"{name}_t{t}", c, piece(t, (mine + 2) % 4), transit.at[t], to(way))

    def sum_near(name, c, t, way, piece, direct, mine, to):
        return copy(f"{name}_d{t}", c, piece(t, (mine - way + 4) % 4), direct.at[t], to(-way))

    def sum_first(name, c, t, way, piece, transit, direct, mine, to):
        return (
            sum_far(name, c, t, way, piece, transit, mine, to),
            sum_near(name, c, t, way, piece, direct, mine, to),
        )

    def sum_second(name, c, t, way, transit, second, to):
        return copy(f"{name}_s{t}", c, transit.at[t], second.at[t], to(way))

    def sum_middle(name, c, piece, transit, direct, second, mine, to):
        for t, way in ways:
            sum_far(name, c, t, way, piece, transit, mine, to).wait_recv()
            transit[t] = (transit[t].astype(F32) + piece(t, (mine + way + 4) % 4)[...].astype(F32)).astype(BF16)
            sum_second(name, c, t, way, transit, second, to).start()

    def sum_last(name, c, piece, transit, direct, second, mine, to):
        totals = []
        for t, way in ways:
            first, straight = sum_first(name, c, t, way, piece, transit, direct, mine, to)
            straight.wait_recv()
            last = sum_second(name, c, t, way, transit, second, to)
            last.wait_recv()
            first.wait_send()
            straight.wait_send()
            last.wait_send()
            totals.append(
                piece(t, mine)[...].astype(F32) + direct[t].astype(F32) + second[t].astype(F32)
            )
        return totals

    def chunk_copy(sem, c, src, dst, to):
        return pltpu.make_async_remote_copy(
            src_ref=src, dst_ref=dst, send_sem=sem.at[0, c], recv_sem=sem.at[1, c],
            device_id=to, device_id_type=MESH,
        )

    def tok_z(step, turn, half):
        c = chunk_of(step, turn, half)
        mine = (ACROSS if turn else OWN)[half]
        return chunk_copy(tok_sem, c, tok.at[:, mine, c0], tok.at[:, c, c0], at_z(-step))

    def tok_y(half):
        c = ACROSS[half]
        return chunk_copy(tok_sem, c, tok.at[:, OWN[half], c0], tok.at[:, c, c0], h_pair)

    def tok_arrived(c):
        here = tok.at[:, c, c0]
        chunk_copy(tok_sem, c, here, here, h_pair).wait_recv()

    def tok_core(c, t):
        here = tok.at[t, c, c0]
        return copy(f"tok_core{t}", c, here, here, c_pair)

    def a_piece(c, t, x):
        return pa.at[c % HELD, t, x]

    def a_args(c):
        s = c % SLOTS
        return functools.partial(a_piece, c), ta.at[s], da.at[s], sa.at[s], x0, at_x

    def a_y(c):
        s = c % SLOTS
        return copy("a_y", c, ya_out.at[s], ya_in.at[s], y_pair)

    def b_y(c, t):
        return copy(f"b_y{t}", c, pb.at[c % HELD, t, 1 - y0], rb.at[c % PAIRED, t], y_pair)

    def b_piece(c, t, x):
        return rb.at[c % PAIRED, t, x]

    def b_args(c):
        s = c % SLOTS
        return functools.partial(b_piece, c), tb.at[s], db.at[s], sb.at[s], x0, at_x

    def ga_y(c):
        here = ha.at[:, c, x0, y0]
        return copy("ga_y", c, here, here, y_pair)

    def gb_y(c, step):
        here = hb.at[:, c, y0, (x0 + step) % 4]
        return copy(f"gb_y{step}", c, here, here, y_pair)

    def ga_first(c):
        return gather_first("ga", c, lambda x: ha.at[:, c, x, y0], x0, at_x)

    def ga_second(c):
        return gather_second("ga", c, lambda t, x: ha.at[t, c, x, y0], x0, at_x, "x")

    def gp_first(c):
        return gather_first("gp", c, lambda x: ha.at[:, c, x, 1 - y0], x0, at_x)

    def gp_second(c):
        return gather_second("gp", c, lambda t, x: ha.at[t, c, x, 1 - y0], x0, at_x, "x")

    def gb_first(c):
        return gather_first("gb", c, lambda x: hb.at[:, c, y0, x], x0, at_x)

    def gb_second(c):
        return gather_second("gb", c, lambda t, x: hb.at[t, c, y0, x], x0, at_x, "x")

    def far_copy(number, src):
        return pltpu.make_async_remote_copy(
            src_ref=src, dst_ref=src, send_sem=far_sem.at[0, number], recv_sem=far_sem.at[1, number],
            device_id=at_x(2), device_id_type=MESH,
        )

    def ga_far():
        return far_copy(0, ha.at[:, last, x0, y0])

    def gp_far():
        return far_copy(1, ha.at[:, last, x0, 1 - y0])

    def gb_far():
        return far_copy(2, hb.at[:, last, y0, x0])

    def o_core(c, t):
        return copy(f"o_core{t}", c, part.at[c % HELD, t, 1 - c0], cr.at[c, t], c_pair)

    def o_z(c):
        step = jnp.where(c < 3, 1, jnp.where(c < 11, (c - 3) // 2, 2 + (c - 11) // 2))
        return chunk_copy(o_sem, c, cr.at[c], zr.at[c], ((z0 + step) % 4, ja, ka))

    def o_y():
        return pltpu.make_async_remote_copy(
            src_ref=yo_out, dst_ref=yo_in, send_sem=y_sem.at[0], recv_sem=y_sem.at[1],
            device_id=h_pair, device_id_type=MESH,
        )

    def start(copies):
        for one in copies:
            one.start()

    def finish(copies):
        for one in copies:
            one.wait_recv()
        for one in copies:
            one.wait_send()

    def wide(c, t):
        return tok[t, c].reshape(-1, tok.shape[-1])

    def gather_tokens_core(c):
        @pl.when(c != OWN[1])
        def _():
            tok_arrived(c)

        start([tok_core(c, t) for t in range(2)])
        for half in halves:
            @pl.when(c == ACROSS[half])
            def _():
                start([tok_z(other, 1, half) for other in (1, 2, 3)])

    def multiply_in(c):
        s = c % HELD
        for t, way in ways:
            finish((tok_core(c, t),))
            if t == 0:
                both = contract(wide(c, 0), u_ref[...], ((1,), (0,)))
            else:
                both = contract(wide(c, 1), w_ref[...], ((1,), (1,)))
            both = both.astype(BF16)
            pa[s, t] = both[:, :WIDE].reshape(pa.shape[2:])
            pb[s, t] = both[:, WIDE:].reshape(pb.shape[2:])
            piece, transit, direct, _, mine, to = a_args(c)
            b_y(c, t).start()
            start(sum_first("a", c, t, way, piece, transit, direct, mine, to))

    def sum_one(c):
        sum_middle("a", c, *a_args(c))
        s = c % SLOTS
        piece, transit, direct, _, mine, to = b_args(c)
        for t, way in ways:
            b_y(c, t).wait_recv()
            here = rb.at[c % PAIRED, t]
            here[...] = (here[...].astype(F32) + pb[c % HELD, t, y0].astype(F32)).astype(BF16)
            start(sum_first("b", c, t, way, piece, transit, direct, mine, to))
        for t in range(2):
            b_y(c, t).wait_send()

    def sum_two(c):
        s = c % SLOTS
        totals = sum_last("a", c, *a_args(c))
        for t in range(2):
            first, second = totals[t][0], totals[t][1]
            ya_own[s, t] = jnp.where(y0 == 0, first, second)
            ya_out[s, t] = jnp.where(y0 == 0, second, first).astype(BF16)
        a_y(c).start()
        sum_middle("b", c, *b_args(c))

    def activate(c):
        s = c % SLOTS
        finish((a_y(c),))
        value, slope = gelu_pair(ya_own[s, 0] + ya_in[s, 0].astype(F32))
        ha[0, c, x0, y0] = value.astype(BF16)
        ha[1, c, x0, y0] = ((ya_own[s, 1] + ya_in[s, 1].astype(F32)) * slope).astype(BF16)
        ga_y(c).start()
        start(ga_first(c))
        totals = sum_last("b", c, *b_args(c))
        value, slope = gelu_pair(totals[0])
        hb[0, c, y0, x0] = value.astype(BF16)
        hb[1, c, y0, x0] = (totals[1] * slope).astype(BF16)
        gb_y(c, 0).start()
        start(gb_first(c))

        @pl.when(c == last)
        def _():
            start((ga_far(), gb_far()))

    def gather_one(c):
        finish((ga_y(c),))
        start(gp_first(c))

        @pl.when(c == last)
        def _():
            gp_far().start()

        finish(gb_first(c))

        @pl.when(c < last)
        def _():
            start(gb_second(c))

        start((gb_y(c, 1), gb_y(c, 3)))

        @pl.when(c == last)
        def _():
            finish((gb_far(),))
            gb_y(c, 2).start()

        finish((gb_y(c, 0),))
        finish(ga_first(c))

        @pl.when(c < last)
        def _():
            start(ga_second(c))

        @pl.when(c == last)
        def _():
            finish((ga_far(),))

    def gather_two(c):
        finish(gp_first(c))
        start(gp_second(c))
        finish(gb_second(c))
        gb_y(c, 2).start()
        finish((gb_y(c, 1), gb_y(c, 3)))

    def multiply_out(c):
        finish(ga_second(c))
        finish(gp_second(c))
        finish((gb_y(c, 2),))
        multiply_gathered(c)

    def multiply_last():
        finish(gp_first(last))
        finish((gp_far(),))
        finish([gb_y(last, step) for step in (1, 2, 3)])
        multiply_gathered(last)

    def multiply_gathered(c):
        s = c % HELD
        for t in range(2):
            left_a = ha[t, c].reshape(-1, ha.shape[-1])
            left_b = hb[t, c].reshape(-1, hb.shape[-1])
            if t == 0:
                both = contract(left_a, w_ref[:WIDE], ((1,), (0,)))
                both += contract(left_b, w_ref[WIDE:], ((1,), (0,)))
            else:
                both = contract(left_a, u_ref[:, :WIDE], ((1,), (1,)))
                both += contract(left_b, u_ref[:, WIDE:], ((1,), (1,)))
            part[s, t] = both.astype(BF16).reshape(part.shape[2:])
            o_core(c, t).start()

    def add_grads(c):
        def add(flat):
            for span, src in zip(spans, (ha, hb)):
                acc_u[:, span] += contract(flat(tok, 0), flat(src, 1), ((0,), (0,)))
                acc_w[span] += contract(flat(src, 0), flat(tok, 1), ((0,), (0,)))

        @pl.when((c % 2 == 1) & (c < last))
        def _():
            add(lambda ref, t: ref[t, pl.ds(c - 1, 2)].reshape(-1, ref.shape[-1]))

        @pl.when(c == last - 1)
        def _():
            add(lambda ref, t: ref[t, c].reshape(-1, ref.shape[-1]))

    def finish_grads():
        def flat(ref, t):
            return ref[t, last].reshape(-1, ref.shape[-1])

        for number, (span, src) in enumerate(zip(spans, (ha, hb))):
            dw_ref[span] = (acc_w[span] + contract(flat(src, 0), flat(tok, 1), ((0,), (0,)))).astype(BF16)
            store_w[number].start()
            du_ref[:, span] = (acc_u[:, span] + contract(flat(tok, 0), flat(src, 1), ((0,), (0,)))).astype(BF16)
            store_u[number].start()

    def total_one(c):
        s = c % HELD
        for t in range(2):
            finish((o_core(c, t),))
            cr[c, t] = (cr[c, t].astype(F32) + part[s, t, c0].astype(F32)).astype(BF16)

    def total_two(c):
        total_one(c)

        @pl.when((c != OWN[0]) & (c != ACROSS[0]) & (c != ACROSS[1]))
        def _():
            o_z(c).start()

    def sum_parts(first, chunks, t):
        total = first.astype(F32)
        for c in chunks:
            total += zr[c, t].astype(F32)
        return total

    def total_across():
        for half in halves:
            chunks = [chunk_of(step, 1, half) for step in (1, 2, 3)]
            for c in chunks:
                o_z(c).wait_recv()
            for t in range(2):
                yo_out[half, t] = sum_parts(cr[ACROSS[half], t], chunks, t).astype(BF16)
        o_y().start()

    def total_own():
        o_y().wait_recv()
        for half in halves:
            chunks = [chunk_of(step, 0, half) for step in (1, 2, 3)]
            for c in chunks:
                o_z(c).wait_recv()
            at = slice(half * rows, (half + 1) * rows)
            for t, ref in enumerate((out_ref, ing_ref)):
                total = sum_parts(cr[OWN[half], t], chunks, t) + yo_in[half, t].astype(F32)
                ref[at, :] = total.astype(BF16)

    stages = (
        (9, total_two), (8, multiply_out), (7, gather_two), (6, gather_one), (5, activate),
        (4, sum_two), (3, sum_one), (1, multiply_in), (0, gather_tokens_core), (8, add_grads),
    )

    start([tok_core(0, t) for t in range(2)])
    start([tok_z(1, 0, half) for half in halves])
    start([tok_y(half) for half in halves])
    start([tok_z(step, 0, half) for step in (2, 3) for half in halves])
    acc_u[...] = jnp.zeros_like(acc_u)
    acc_w[...] = jnp.zeros_like(acc_w)
    load_u.wait()
    load_w.wait()

    def step(number, carry):
        for behind, stage in stages:
            begin = 1 if stage is gather_tokens_core else behind

            count = CHUNKS - 1 if stage is gather_two else CHUNKS

            @pl.when((number >= begin) & (number < behind + count))
            def _():
                stage(number - behind)

        @pl.when(number == chunk_of(3, 1, 1) + 11)
        def _():
            total_across()

        return carry

    lax.fori_loop(0, CHUNKS + 7, step, 0)
    total_two(last - 1)
    multiply_last()
    finish_grads()
    total_one(last)
    total_own()
    for half in halves:
        tok_y(half).wait_send()
        for other in (1, 2, 3):
            tok_z(other, 0, half).wait_send()
            tok_z(other, 1, half).wait_send()
            o_z(chunk_of(other, 0, half)).wait_send()
            o_z(chunk_of(other, 1, half)).wait_send()
    o_y().wait_send()
    for one in store_u + store_w:
        one.wait()


def hand_on(*refs):
    sources, targets, held, sem = refs[:4], refs[4:8], refs[8:12], refs[12]
    copies = []
    for source, target, room in zip(sources, targets, held):
        parts = max(1, source.shape[0] // 384)
        rows = source.shape[0] // parts
        for number in range(parts):
            at = pl.ds(number * rows, rows)
            place = len(copies)
            copies.append((
                pltpu.make_async_copy(source.at[at], room.at[at], sem.at[0, place]),
                pltpu.make_async_copy(room.at[at], target.at[at], sem.at[1, place]),
            ))
    for load, _ in copies:
        load.start()
    for load, store in copies:
        load.wait()
        store.start()
    for _, store in copies:
        store.wait()


def per_device(inputs, up_weight, down_weight, out_grad):
    tokens, width = inputs.shape
    hidden = up_weight.shape[1]
    rows = tokens // 2
    owned = rows // 4
    narrow = hidden - WIDE

    def vmem(*shape, dtype=BF16):
        return pltpu.VMEM(shape, dtype)

    scratch = [
        vmem(width, hidden),
        vmem(hidden, width),
        vmem(width, hidden),
        vmem(hidden, width),
        pltpu.SemaphoreType.DMA((5, 2)),
        vmem(2, CHUNKS, 2, rows, width),
        vmem(HELD, 2, 4, 2, owned, WIDE),
        vmem(HELD, 2, 2, 4, owned, narrow),
        *[vmem(SLOTS, 2, 2, owned, WIDE)] * 3,
        vmem(SLOTS, 2, owned, WIDE),
        vmem(SLOTS, 2, owned, WIDE),
        vmem(SLOTS, 2, owned, WIDE, dtype=F32),
        vmem(PAIRED, 2, 4, owned, narrow),
        *[vmem(SLOTS, 2, owned, narrow)] * 3,
        vmem(2, CHUNKS, 4, 2, owned, WIDE),
        vmem(2, CHUNKS, 2, 4, owned, narrow),
        vmem(HELD, 2, 2, rows, width),
        vmem(CHUNKS, 2, rows, width),
        vmem(CHUNKS, 2, rows, width),
        vmem(2, 2, rows, width),
        vmem(2, 2, rows, width),
        vmem(width, hidden, dtype=F32),
        vmem(hidden, width, dtype=F32),
        pltpu.SemaphoreType.DMA((len(NAMES) * SENT + len(EARLY),)),
        pltpu.SemaphoreType.DMA((len(NAMES) * RECEIVED + len(EARLY),)),
        *[pltpu.SemaphoreType.DMA((2, CHUNKS))] * 2,
        pltpu.SemaphoreType.DMA((2,)),
        pltpu.SemaphoreType.DMA((2, 3)),
    ]
    results = (
        jax.ShapeDtypeStruct(inputs.shape, BF16),
        jax.ShapeDtypeStruct(inputs.shape, BF16),
        jax.ShapeDtypeStruct(up_weight.shape, BF16),
        jax.ShapeDtypeStruct(down_weight.shape, BF16),
    )
    near, far = pl.BlockSpec(memory_space=pltpu.VMEM), pl.BlockSpec(memory_space=pl.ANY)
    made = pl.pallas_call(
        kernel,
        out_shape=results,
        in_specs=[far] * 4,
        out_specs=[near, near, far, far],
        scratch_shapes=scratch,
        compiler_params=pltpu.CompilerParams(
            collective_id=0, has_side_effects=True, vmem_limit_bytes=62 * 1024 * 1024
        ),
    )(
        inputs.reshape(2, rows, width), up_weight, down_weight,
        out_grad.reshape(2, rows, width),
    )
    return pl.pallas_call(
        hand_on,
        out_shape=results,
        in_specs=[far] * 4,
        out_specs=[far] * 4,
        scratch_shapes=[vmem(*one.shape) for one in results] + [pltpu.SemaphoreType.DMA((2, 8))],
        compiler_params=pltpu.CompilerParams(vmem_limit_bytes=62 * 1024 * 1024),
    )(*made)


def solution(mesh):
    placed = (
        P(("ia", "ka"), "ja"),
        P("ja", ("ka", "ia")),
        P(("ka", "ia"), "ja"),
        P(("ia", "ka"), "ja"),
    )
    return jax.shard_map(
        per_device,
        mesh=mesh,
        in_specs=placed,
        out_specs=(
            P(("ia", "ka"), "ja"),
            P(("ia", "ka"), "ja"),
            P("ja", ("ka", "ia")),
            P(("ka", "ia"), "ja"),
        ),
        check_vma=False,
    )
```
